256 devices in a mesh: leaf: 16 (over z, core), front: 16 (over x, y).
Axes of the slice: x: 4, y: 4, z: 8, core: 2. Of those that a mesh axis runs over, the one named last changes fastest.
Arguments:
- rhs_leaf: float32 [16, 1024, 256], P('leaf', 'front'), may hold values from -6 to 6
- rhs_top: float32 [15, 1024, 256], P(None, 'front'), may hold values from -6 to 6
- inv_leaf: bfloat16 [16, 1024, 1024], P('leaf', 'front'), as said below
- inv_top: bfloat16 [15, 1024, 1024], P(None, 'front'), as said below
- off_leaf: bfloat16 [16, 1024, 1024], P('leaf', None, 'front'), may hold values from -0.09375 to 0.09375
- off_top: bfloat16 [14, 1024, 1024], P(None, None, 'front'), may hold values from -0.09375 to 0.09375
- idx_leaf: int32 [16, 1024], P('leaf'), may hold values from 0 to 4095, as said below
- idx_top: int32 [14, 1024], replicated, may hold values from 0 to 3071, as said below
Outputs:
- leaf_solution: float32 [16, 1024, 256], P('leaf', 'front')
- ancestor_solution: float32 [16, 4, 1024, 256], P('leaf', None, 'front')
The draws below stay inside these ranges and needn't reach their ends.
Inputs may be any that keep to these rules, and one draw needn't show every extreme that they name: `idx_leaf`: entry r of row g is a * 1024 + q with a < 4: update row r of split-level front g lands on row q of its depth-a ancestor. `idx_top`: row j belongs to the upper front with heap number h = j + 2; its entries are a * 1024 + q with a < floor(log2 h): update row r lands on row q of h's depth-a ancestor. `inv_leaf`: every block is lower triangular with a positive diagonal. `inv_top`: every block is lower triangular with a positive diagonal.
All inputs are finite; a program needn't handle non-finite values.
Results may differ from the reference program's by a relative error of at most 0.0055.
Values may be sent and summed in bfloat16 or wider, within the bound.
No kernel may reach another device: no remote copies, remote signals or barrier semaphores. Data moves between devices by JAX's collectives and lax.ppermute only.
A program may use at most 64 MiB of HBM per device.

```python
import jax
import jax.numpy as jnp
import numpy as np
from jax import lax

S = 1024
R = 1024
NRHS = 256
TOPS = 15
LEVELS = 4


def lower_inverse(key, count):
    key_off, key_diag = jax.random.split(key)
    below = jax.random.normal(key_off, (count, S, S), jnp.float32) / jnp.sqrt(jnp.float32(S))
    diag_vals = jax.random.uniform(key_diag, (count, S), jnp.float32, minval=0.5, maxval=2.0)
    row_ids = jnp.arange(S)[:, None]
    col_ids = jnp.arange(S)[None, :]
    lower = jnp.where(col_ids < row_ids, below, 0.0)
    on_diag = jnp.where(col_ids == row_ids, diag_vals[:, :, None], 0.0)
    return (lower + on_diag).astype(jnp.bfloat16)


def draw_inv_leaf(key, part):
    key = jax.random.fold_in(key, 11)
    return lower_inverse(key, TOPS + 1)


def draw_inv_top(key, part):
    key = jax.random.fold_in(key, 12)
    return lower_inverse(key, TOPS)


def draw_idx_leaf(key, part):
    key = jax.random.fold_in(key, 13)
    values = jax.random.randint(key, (TOPS + 1, R), 0, LEVELS * S, dtype=jnp.int32)
    values = values.at[0, 0].set(LEVELS * S - 1)
    values = values.at[0, 1].set(0)
    return values


def draw_idx_top(key, part):
    key = jax.random.fold_in(key, 14)
    heap_ids = jnp.arange(TOPS - 1, dtype=jnp.int32) + 2
    depth_total = jnp.zeros((TOPS - 1,), jnp.int32)
    for power in range(1, 9):
        depth_total = depth_total + (heap_ids >= 2 ** power).astype(jnp.int32)
    span = depth_total * S
    raw_values = jax.random.randint(key, (TOPS - 1, R), 0, 2 ** 24, dtype=jnp.int32)
    values = raw_values % span[:, None]
    values = values.at[TOPS - 2, 0].set(span[TOPS - 2] - 1)
    values = values.at[0, 1].set(0)
    return values


def shard_levels(stream_key, dims, pieces, least, largest):
    factor_of, own = 1.0, jax.random.fold_in(stream_key, 6)
    for axis_at, blocks in pieces:
        draws = jnp.exp(jax.random.uniform(jax.random.fold_in(own, axis_at), (blocks,), jnp.float32, least / len(pieces), largest / len(pieces)))
        factor_of = factor_of * jnp.repeat(draws, dims[axis_at] // blocks).reshape([-1 if axis == axis_at else 1 for axis in range(len(dims))])
    return factor_of


def normal_values(own_key, shape, width, most, cuts=(), kind=jnp.bfloat16):
    result = width * jax.random.normal(own_key, shape, jnp.float32)
    if cuts:
        result = result * shard_levels(own_key, shape, cuts, -0.22, 0.18)
    return jnp.clip(result, -most, most).astype(kind)


def setup_inputs(seed: int = 0) -> dict:
    splits = jax.random.split(jax.random.key(seed), 9)
    rhs_leaf = normal_values(splits[0], (TOPS + 1, S, NRHS), 1.0, 6.0, ((0, 16), (1, 16)), jnp.float32)
    rhs_top = normal_values(splits[1], (TOPS, S, NRHS), 1.0, 6.0, ((1, 16),), jnp.float32)
    inv_leaf = draw_inv_leaf(jax.random.fold_in(splits[8], 71), 0)
    inv_top = draw_inv_top(jax.random.fold_in(splits[8], 71), 0)
    off_leaf = normal_values(splits[4], (TOPS + 1, R, S), (4 * S) ** -0.5, 0.09375, ((0, 16), (2, 16)))
    off_top = normal_values(splits[5], (TOPS - 1, R, S), (4 * S) ** -0.5, 0.09375, ((2, 16),))
    idx_leaf = draw_idx_leaf(jax.random.fold_in(splits[8], 71), 0)
    idx_top = draw_idx_top(jax.random.fold_in(splits[8], 71), 0)
    return {"rhs_leaf": rhs_leaf, "rhs_top": rhs_top, "inv_leaf": inv_leaf, "inv_top": inv_top, "off_leaf": off_leaf, "off_top": off_top, "idx_leaf": idx_leaf, "idx_top": idx_top}


def apply_inverse(inverse, right_side):
    rounded = lax.optimization_barrier(right_side.astype(jnp.bfloat16)).astype(jnp.float32)
    return jnp.einsum("nij,njk->nik", inverse.astype(jnp.float32), rounded, precision=lax.Precision.HIGHEST)


def push_updates(pending, off_block, solution, row_list, owners):
    rounded = lax.optimization_barrier(solution.astype(jnp.bfloat16)).astype(jnp.float32)
    updates = jnp.einsum("nrs,nsk->nrk", off_block.astype(jnp.float32), rounded, precision=lax.Precision.HIGHEST)
    depth_idx = row_list // S
    target_row = row_list % S
    heap_node = jnp.right_shift(owners[:, None], depth_idx + 1)
    flat_index = ((heap_node - 1) * S + target_row).reshape(-1).astype(jnp.int32)
    return pending + jax.ops.segment_sum(updates.reshape(-1, NRHS), flat_index, num_segments=TOPS * S)


def reference(rhs_leaf, rhs_top, inv_leaf, inv_top, off_leaf, off_top, idx_leaf, idx_top):
    leaf_count = TOPS + 1
    leaf_solution = apply_inverse(inv_leaf, rhs_leaf)
    pending = jnp.zeros((TOPS * S, NRHS), jnp.float32)
    owners = (leaf_count + jnp.arange(leaf_count)).astype(jnp.int32)
    pending = push_updates(pending, off_leaf, leaf_solution, idx_leaf, owners)
    solved = {}
    for level_num in range(LEVELS - 1, -1, -1):
        first_node = 2 ** level_num
        end_node = 2 ** (level_num + 1)
        collected = pending.reshape(TOPS, S, NRHS)[first_node - 1:end_node - 1]
        reduced = rhs_top[first_node - 1:end_node - 1] - collected
        solution = apply_inverse(inv_top[first_node - 1:end_node - 1], reduced)
        solved[level_num] = solution
        if level_num > 0:
            heap_ids = jnp.arange(first_node, end_node).astype(jnp.int32)
            pending = push_updates(pending, off_top[first_node - 2:end_node - 2], solution, idx_top[first_node - 2:end_node - 2], heap_ids)
    top_solution = jnp.concatenate([solved[level_num] for level_num in range(LEVELS)], axis=0)
    table_index = np.array([[((leaf_count + g) >> (a + 1)) - 1 for a in range(LEVELS)] for g in range(leaf_count)], dtype=np.int32)
    ancestor_solution = top_solution[jnp.asarray(table_index)]
    return (leaf_solution, ancestor_solution)
```

```python
import functools

import jax
import jax.numpy as jnp
from jax import lax
from jax.experimental import pallas as pl
from jax.experimental.pallas import tpu as pltpu
from jax.sharding import PartitionSpec as P

BF = jnp.bfloat16
F32 = jnp.float32
FRONTS = 16
COLS = 16
WIDTHS = (8, 4, 2, 1)
STARTS = (0, 8, 12, 14)

VMEM = pl.BlockSpec(memory_space=pltpu.VMEM)
SMEM = pl.BlockSpec(memory_space=pltpu.SMEM)


def nt(a, b):
    return lax.dot_general(a, b, (((1,), (1,)), ((), ())), preferred_element_type=F32)


def nn(a, b):
    return jnp.dot(a, b, preferred_element_type=F32)


def halves(value):
    high = value.astype(BF)
    low = (value - high.astype(F32)).astype(BF)
    return high, low


def iota(shape, dim):
    return lax.broadcasted_iota(jnp.int32, shape, dim)


def params():
    return pltpu.CompilerParams(vmem_limit_bytes=40 * 2**20)


def call(kernel, outs, specs, args, flops=10**8, bytes_accessed=10**6):
    many = isinstance(outs, (tuple, list))
    return pl.pallas_call(
        kernel,
        out_shape=outs,
        in_specs=specs,
        out_specs=tuple(VMEM for _ in outs) if many else VMEM,
        compiler_params=params(),
        cost_estimate=pl.CostEstimate(
            flops=flops, bytes_accessed=bytes_accessed, transcendentals=0
        ),
    )(*args)


def weights_kernel(place, inv_ref, off_ref, out_ref):
    core = place[8]
    rows = inv_ref.shape[1]
    out_ref[:rows, :] = inv_ref[0]
    pick = (iota((rows, 2 * rows), 1) == iota((rows, 2 * rows), 0) + core * rows).astype(BF)
    out_ref[rows:, :] = nt(pick, off_ref[0]).astype(BF)


def path_weights(place, inv_top, off_top, levels):
    width = inv_top.shape[2]
    rows = inv_top.shape[1] // 2
    return pl.pallas_call(
        weights_kernel,
        grid_spec=pltpu.PrefetchScalarGridSpec(
            num_scalar_prefetch=1,
            grid=(levels,),
            in_specs=[
                pl.BlockSpec((1, rows, width), lambda a, s: (s[a] - 1, s[8], 0)),
                pl.BlockSpec((1, width, 2 * rows), lambda a, s: (s[a] - 2, 0, 0)),
            ],
            out_specs=pl.BlockSpec((2 * rows, width), lambda a, s: (a, 0)),
        ),
        out_shape=jax.ShapeDtypeStruct((levels * 2 * rows, width), BF),
        compiler_params=params(),
    )(place, inv_top, off_top)


def shares_kernel(place, *refs):
    rhs_refs, out_ref = refs[:4], refs[4]
    parity = place[9]
    total = jnp.zeros(out_ref.shape, F32)
    to = iota((256, 256), 0)
    come = iota((256, 256), 1)
    slot = to % 16
    for a in range(4):
        sub = place[4 + a]
        width, start = WIDTHS[a], STARTS[a]
        from_col = (to - slot) + sub * width + (slot - start)
        chosen = (slot >= start) & (slot < start + width) & (come == from_col)
        high, low = halves(rhs_refs[a][0])
        high = high.astype(F32)
        low = low.astype(F32)
        even = (parity == 0).astype(F32)
        odd = 1.0 - even
        stacked = jnp.concatenate([high * even, high * odd, low * even, low * odd], axis=0)
        total = total + nt(chosen.astype(BF), stacked.astype(BF))
    out_ref[...] = total.astype(BF)


def rhs_shares(place, rhs_top):
    rows, cols = rhs_top.shape[1:]
    return pl.pallas_call(
        shares_kernel,
        grid_spec=pltpu.PrefetchScalarGridSpec(
            num_scalar_prefetch=1,
            grid=(1,),
            in_specs=[
                pl.BlockSpec((1, rows, cols), lambda i, s, a=a: (s[a] - 1, 0, 0)) for a in range(4)
            ],
            out_specs=pl.BlockSpec((256, 256), lambda i, s: (0, 0)),
        ),
        out_shape=jax.ShapeDtypeStruct((256, 256), BF),
        compiler_params=params(),
    )(place, rhs_top, rhs_top, rhs_top, rhs_top)


def leaf_solve_kernel(inv_ref, rhs_ref, off_ref, shares_ref, x_ref, out_ref):
    right = rhs_ref[...].reshape(1024, 256)
    x = nn(inv_ref[0], right)
    x_ref[...] = x
    xt = x.T.astype(BF)
    update = nt(xt, off_ref[0])
    out_ref[:, :, :1024] = update.astype(BF).reshape(16, 16, 1024)
    out_ref[:, :, 1024:] = shares_ref[...].reshape(16, 16, 256)


def push(update, idx, count):
    high, low = halves(update)
    both = jnp.concatenate([high, low], axis=0)
    blocks = []
    step = 512
    for a in range(count):
        parts = []
        for t in range(1024 // step):
            hit = iota((step, 1024), 0) + (a * 1024 + t * step) == idx
            got = nt(both, jnp.where(hit, 1.0, 0.0).astype(BF))
            parts.append(got[:16] + got[16:])
        blocks.append(jnp.concatenate(parts, axis=1))
    return blocks


def leaf_update_kernel(place, got_ref, idx_ref, out_ref):
    update = jnp.zeros((16, 1024), F32)
    for s in range(FRONTS):
        update = update + got_ref[s, :, :1024].astype(F32)
    pending = push(update, idx_ref[...], 4)
    high, low = [], []
    for g in range(FRONTS // 2):
        pair = got_ref[2 * g, :, 1024:].astype(F32) + got_ref[2 * g + 1, :, 1024:].astype(F32)
        high.append(pair[:, :128])
        low.append(pair[:, 128:])
    high = jnp.concatenate(high, axis=1).astype(BF)
    low = jnp.concatenate(low, axis=1).astype(BF)
    row = iota((16, 16), 0)
    slot = iota((16, 16), 1)
    for a in range(4):
        width, start = WIDTHS[a], STARTS[a]
        put = (slot >= start) & (slot < start + width)
        put = put & (row == place[4 + a] * width + slot - start)
        put = jnp.where(put, 1.0, 0.0).astype(BF)
        out_ref[a * 16 : (a + 1) * 16, :] = nn(put, high) + nn(put, low) - pending[a]


def solve_kernel(left, own_ref, other_ref, weights_ref, ux_ref, *rest):
    total = own_ref[...] + other_ref[...]
    right = total[:16].astype(BF)
    inverse = weights_ref[:, :32, :].reshape(512, 1024)
    off = weights_ref[:, 32:, :].reshape(512, 1024)
    x = nt(right, inverse)
    ux_ref[:, :1024] = nn(x.astype(BF), off)
    ux_ref[:, 1024:] = x
    rest[0][...] = total[16:]


def top_solve(own, other, weights, level):
    left = own.shape[0] // 16 - 1
    return pl.pallas_call(
        functools.partial(solve_kernel, left),
        grid=(1,),
        in_specs=[
            pl.BlockSpec(own.shape, lambda i: (0, 0)),
            pl.BlockSpec(own.shape, lambda i: (0, 0)),
            pl.BlockSpec((16, 64, 1024), lambda i: (0, level, 0)),
        ],
        out_specs=(
            pl.BlockSpec((16, 1536), lambda i: (0, 0)),
            pl.BlockSpec((left * 16, 1024), lambda i: (0, 0)),
        ),
        out_shape=(
            jax.ShapeDtypeStruct((16, 1536), F32),
            jax.ShapeDtypeStruct((left * 16, 1024), F32),
        ),
        compiler_params=params(),
    )(own, other, weights)


def update_kernel(own_ref, other_ref, rest_ref, idx_ref, out_ref):
    update = own_ref[:, :1024] + other_ref[:, :1024]
    count = out_ref.shape[0] // 16
    for a, block in enumerate(push(update, idx_ref[...], count)):
        out_ref[a * 16 : (a + 1) * 16, :] = rest_ref[a * 16 : (a + 1) * 16, :] - block


def ship_kernel(place, own_ref, other_ref, out_ref):
    first = place[8] == 0
    own = own_ref[:, 1024:]
    other = other_ref[:, 1024:]
    low_core = jnp.where(first, own, other)
    high_core = jnp.where(first, other, own)
    for f in range(FRONTS):
        at = slice(f * 32, (f + 1) * 32)
        value = jnp.concatenate([low_core[:, at], high_core[:, at]], axis=1)
        high = value.astype(BF).astype(F32)
        low = value - high
        out_ref[f] = jnp.concatenate([high, low], axis=1).astype(BF)


def root_right_kernel(own_ref, other_ref, s3_ref, s2_ref, s1_ref, out_ref):
    right = (own_ref[...] + other_ref[...]).astype(BF)
    for f in range(FRONTS):
        out_ref[f, :, :1024] = right
    out_ref[:, :, 1024:1152] = s3_ref[...]
    out_ref[:, :, 1152:1280] = s2_ref[...]
    out_ref[:, :, 1280:] = s1_ref[...]


def root_kernel(got_ref, inv_ref, out_ref):
    right = got_ref[:, :, :1024].reshape(256, 1024)
    out_ref[3] = nt(inv_ref[0], right)
    for a in range(3):
        at = 1024 + a * 128
        both = got_ref[:, :, at : at + 128].reshape(256, 128).astype(F32).T
        out_ref[a] = both[:64] + both[64:]


def swap(block, pairs):
    return lax.ppermute(block, "leaf", pairs)


def core_pairs():
    return [(i, i ^ 1) for i in range(16)]


def chip_pairs(level):
    pairs = []
    for i in range(16):
        z, core = i // 2, i % 2
        if level == 0:
            to = z ^ 1
        elif level == 1:
            to = z ^ 2
        else:
            to = (6, 7, 4, 5, 2, 3, 0, 1)[z]
        pairs.append((i, 2 * to + core))
    return pairs


def local(rhs_leaf, rhs_top, inv_leaf, inv_top, off_leaf, off_top, idx_leaf, idx_top):
    leaf = lax.axis_index("leaf")
    front = lax.axis_index("front")
    nodes = [jnp.right_shift(16 + leaf, a + 1) for a in range(4)]
    subs = [leaf & (2 ** (a + 1) - 1) for a in range(4)]
    place = jnp.stack(nodes + subs + [leaf & 1, front & 1]).astype(jnp.int32)

    rounded = rhs_leaf[0].astype(BF)
    sent = jnp.broadcast_to(rounded[None], (FRONTS, *rounded.shape))
    right = lax.all_to_all(sent, "front", 0, 0)

    path = path_weights(place, inv_top, off_top, 3)
    weights = lax.all_gather(path, "front", axis=0, tiled=False)
    shares = rhs_shares(place, rhs_top)

    leaf_x, sent = call(
        leaf_solve_kernel,
        (jax.ShapeDtypeStruct((64, 256), F32), jax.ShapeDtypeStruct((16, 16, 1280), BF)),
        [VMEM] * 4,
        (inv_leaf, right, off_leaf, shares),
    )
    got = lax.all_to_all(sent, "front", 0, 0)
    state = call(
        leaf_update_kernel,
        jax.ShapeDtypeStruct((64, 1024), F32),
        [SMEM, VMEM, VMEM],
        (place, got, idx_leaf),
    )
    other = swap(state, core_pairs())
    ships = []
    for level in range(3):
        ux, rest = top_solve(state, other, weights, level)
        ux_other = swap(ux, core_pairs())
        rows = lax.dynamic_slice_in_dim(idx_top, nodes[level] - 2, 1, 0)
        state = call(
            update_kernel,
            jax.ShapeDtypeStruct(rest.shape, F32),
            [VMEM] * 4,
            (ux, ux_other, rest, rows),
        )
        other = swap(state, chip_pairs(level))
        ships.append(
            call(
                ship_kernel,
                jax.ShapeDtypeStruct((16, 16, 128), BF),
                [SMEM, VMEM, VMEM],
                (place, ux, ux_other),
            )
        )
    sent = call(
        root_right_kernel,
        jax.ShapeDtypeStruct((16, 16, 1408), BF),
        [VMEM] * 5,
        (state, other, *ships),
    )
    got = lax.all_to_all(sent, "front", 0, 0)
    ancestors = call(
        root_kernel,
        jax.ShapeDtypeStruct((4, 64, 256), F32),
        [VMEM] * 2,
        (got, inv_top[:1]),
    )
    return (leaf_x[None], ancestors[None])


def solution(mesh):
    placed = (
        P("leaf", "front", None),
        P(None, "front", None),
        P("leaf", "front", None),
        P(None, "front", None),
        P("leaf", None, "front"),
        P(None, None, "front"),
        P("leaf", None),
        P(),
    )
    return jax.shard_map(
        local,
        mesh=mesh,
        in_specs=placed,
        out_specs=(P("leaf", "front", None), P("leaf", None, "front", None)),
        check_vma=False,
    )
```

```python
import functools

import jax
import jax.numpy as jnp
from jax import lax
from jax.experimental import pallas as pl
from jax.experimental.pallas import tpu as pltpu
from jax.sharding import PartitionSpec as P

BF = jnp.bfloat16
F32 = jnp.float32
FRONTS = 16
COLS = 16
WIDTHS = (8, 4, 2, 1)
STARTS = (0, 8, 12, 14)

VMEM = pl.BlockSpec(memory_space=pltpu.VMEM)
SMEM = pl.BlockSpec(memory_space=pltpu.SMEM)
HBM = pl.BlockSpec(memory_space=pltpu.HBM)


def nt(a, b):
    return lax.dot_general(a, b, (((1,), (1,)), ((), ())), preferred_element_type=F32)


def nn(a, b):
    return jnp.dot(a, b, preferred_element_type=F32)


def halves(value):
    high = value.astype(BF)
    low = (value - high.astype(F32)).astype(BF)
    return high, low


def iota(shape, dim):
    return lax.broadcasted_iota(jnp.int32, shape, dim)


def params(mib=16):
    return pltpu.CompilerParams(vmem_limit_bytes=mib * 2**20)


def call(kernel, outs, specs, args, flops=10**8, bytes_accessed=10**6):
    many = isinstance(outs, (tuple, list))
    return pl.pallas_call(
        kernel,
        out_shape=outs,
        in_specs=specs,
        out_specs=tuple(VMEM for _ in outs) if many else VMEM,
        compiler_params=params(),
        cost_estimate=pl.CostEstimate(
            flops=flops, bytes_accessed=bytes_accessed, transcendentals=0
        ),
    )(*args)


def weights_kernel(place, inv_ref, off_ref, out_ref, held, sems):
    level = pl.program_id(0)
    node = place[level]
    at = pl.ds(pl.multiple_of(place[8] * 32, 32), 32)
    copies = [
        pltpu.make_async_copy(inv_ref.at[node - 1, at, :], held.at[0], sems.at[0]),
        pltpu.make_async_copy(off_ref.at[node - 2, at, :], held.at[1], sems.at[1]),
    ]
    for copy in copies:
        copy.start()
    for copy in copies:
        copy.wait()
    for f in range(FRONTS):
        out_ref[f, :32, :] = held[0]
        out_ref[f, 32:, :] = held[1]


def path_weights(place, inv_top, off_top, levels):
    return pl.pallas_call(
        weights_kernel,
        grid=(levels,),
        out_shape=jax.ShapeDtypeStruct((FRONTS, levels * 64, 1024), BF),
        in_specs=[SMEM, HBM, HBM],
        out_specs=pl.BlockSpec((FRONTS, 64, 1024), lambda i: (0, i, 0)),
        scratch_shapes=[pltpu.VMEM((2, 32, 1024), BF), pltpu.SemaphoreType.DMA((2,))],
        compiler_params=params(60),
    )(place, inv_top, off_top)


def shares_kernel(place, rhs_ref, out_ref, held, sems):
    copies = [
        pltpu.make_async_copy(rhs_ref.at[place[a] - 1], held.at[a], sems.at[a]) for a in range(4)
    ]
    for copy in copies:
        copy.start()
    for copy in copies:
        copy.wait()
    total = jnp.zeros((256, 128), F32)
    to = iota((256, 256), 0)
    come = iota((256, 256), 1)
    slot = to % 16
    for a in range(4):
        sub = place[4 + a]
        width, start = WIDTHS[a], STARTS[a]
        from_col = (to - slot) + sub * width + (slot - start)
        chosen = (slot >= start) & (slot < start + width) & (come == from_col)
        stacked = jnp.concatenate(halves(held[a]), axis=0)
        total = total + nt(jnp.where(chosen, 1.0, 0.0).astype(BF), stacked)
    out_ref[...] = total.astype(BF).reshape(4, 64, 128)


def rhs_shares(place, rhs_top):
    return pl.pallas_call(
        shares_kernel,
        out_shape=jax.ShapeDtypeStruct((4, 64, 128), BF),
        in_specs=[SMEM, HBM],
        out_specs=VMEM,
        scratch_shapes=[pltpu.VMEM((4, 64, 256), F32), pltpu.SemaphoreType.DMA((4,))],
        compiler_params=params(60),
    )(place, rhs_top)


def leaf_solve_kernel(place, inv_ref, r0, r1, r2, r3, off_ref, shares_ref, *refs):
    x_ref, outs, right_ref, update_ref = refs[0], refs[1:5], refs[5], refs[6]
    front_x, front_y = place[9], place[10]
    for t, r in enumerate((r0, r1, r2, r3)):
        for s in range(4):
            right_ref[(front_x ^ t) * 4 + (front_y ^ s)] = r[s]
    right = right_ref[...].reshape(1024, 256)
    x = nn(inv_ref[0], right)
    x_ref[...] = x
    xt = x.T.astype(BF)
    update_ref[...] = nn(xt, off_ref[0]).astype(BF).reshape(4, 64, 1024)
    for t, out_ref in enumerate(outs):
        to = front_x ^ t
        out_ref[:, :1024] = update_ref[to]
        out_ref[:, 1024:] = shares_ref[to]


def fold_kernel(place, r0, r1, r2, r3, *outs):
    front_x, front_y = place[9], place[10]
    refs = (r0, r1, r2, r3)
    for s, out_ref in enumerate(outs):
        at = pl.ds(pl.multiple_of((front_y ^ s) * 16, 16), 16)
        total = refs[0][at, :1024].astype(F32)
        for r in refs[1:]:
            total = total + r[at, :1024].astype(F32)
        out_ref[:, :1024] = total
        for t, r in enumerate(refs):
            both = r[at, 1024:].astype(F32)
            share = both + pltpu.roll(both, 64, 1)
            lanes = pl.ds(pl.multiple_of((1024 + (front_x ^ t) * 128), 128), 128)
            out_ref[:, lanes] = share


def push(update, idx, count):
    high, low = halves(update)
    both = jnp.concatenate([high, low], axis=0)
    blocks = []
    step = 512
    for a in range(count):
        parts = []
        for t in range(1024 // step):
            hit = iota((step, 1024), 0) + (a * 1024 + t * step) == idx
            got = nt(both, jnp.where(hit, 1.0, 0.0).astype(BF))
            parts.append(got[:16] + got[16:])
        blocks.append(jnp.concatenate(parts, axis=1))
    return blocks


def leaf_update_kernel(place, r0, r1, r2, r3, idx_ref, out_ref, held):
    front_y = place[10]
    refs = (r0, r1, r2, r3)
    update = refs[0][:, :1024]
    for r in refs[1:]:
        update = update + r[:, :1024]
    pending = push(update, idx_ref[...], 4)
    for s, r in enumerate(refs):
        held[front_y ^ s] = r[:, 1024:]
    pieces = []
    left_half = iota((16, 128), 1) < 64
    for x in range(4):
        at = slice(x * 128, (x + 1) * 128)
        for y in (0, 2):
            pieces.append(jnp.where(left_half, held[y][:, at], held[y + 1][:, at]))
    shares = jnp.concatenate(pieces, axis=1)
    high, low = halves(shares)
    row = iota((16, 16), 0)
    slot = iota((16, 16), 1)
    for a in range(4):
        width, start = WIDTHS[a], STARTS[a]
        put = (slot >= start) & (slot < start + width)
        put = put & (row == place[4 + a] * width + slot - start)
        put = jnp.where(put, 1.0, 0.0).astype(BF)
        out_ref[a * 16 : (a + 1) * 16, :] = nn(put, high) + nn(put, low) - pending[a]


def solve_kernel(own_ref, other_ref, weights_ref, ux_ref, rest_ref):
    total = own_ref[...] + other_ref[...]
    right = total[:16].astype(BF)
    inverse = weights_ref[:, :32, :].reshape(512, 1024)
    off = weights_ref[:, 32:, :].reshape(512, 1024)
    x = nt(right, inverse)
    ux_ref[:, :1024] = nn(x.astype(BF), off)
    ux_ref[:, 1024:] = x
    rest_ref[...] = total[16:]


def top_solve(own, other, weights, level):
    left = own.shape[0] - 16
    whole = pl.BlockSpec(own.shape, lambda i: (0, 0))
    return pl.pallas_call(
        solve_kernel,
        grid=(1,),
        in_specs=[whole, whole, pl.BlockSpec((FRONTS, 64, 1024), lambda i: (0, level, 0))],
        out_specs=(
            pl.BlockSpec((16, 1536), lambda i: (0, 0)),
            pl.BlockSpec((left, 1024), lambda i: (0, 0)),
        ),
        out_shape=(jax.ShapeDtypeStruct((16, 1536), F32), jax.ShapeDtypeStruct((left, 1024), F32)),
        compiler_params=params(),
    )(own, other, weights)


def update_kernel(level, place, own_ref, other_ref, rest_ref, idx_ref, out_ref):
    update = own_ref[:, :1024] + other_ref[:, :1024]
    count = out_ref.shape[0] // 16
    idx = idx_ref[pl.ds(place[level] - 2, 1), :]
    for a, block in enumerate(push(update, idx, count)):
        out_ref[a * 16 : (a + 1) * 16, :] = rest_ref[a * 16 : (a + 1) * 16, :] - block


def ship_kernel(place, own_ref, other_ref, out_ref):
    first = place[8] == 0
    own = own_ref[:, 1024:]
    other = other_ref[:, 1024:]
    low_core = jnp.where(first, own, other)
    high_core = jnp.where(first, other, own)
    for f in range(FRONTS):
        at = slice(f * 32, (f + 1) * 32)
        value = jnp.concatenate([low_core[:, at], high_core[:, at]], axis=1)
        high = value.astype(BF).astype(F32)
        low = value - high
        out_ref[f] = jnp.concatenate([high, low], axis=1).astype(BF)


def root_right_kernel(own_ref, other_ref, s3_ref, s2_ref, s1_ref, out_ref):
    right = (own_ref[...] + other_ref[...]).astype(BF)
    for f in range(FRONTS):
        out_ref[f, :, :1024] = right
    out_ref[:, :, 1024:1152] = s3_ref[...]
    out_ref[:, :, 1152:1280] = s2_ref[...]
    out_ref[:, :, 1280:] = s1_ref[...]


def root_kernel(got_ref, inv_ref, out_ref):
    right = got_ref[:, :, :1024].reshape(256, 1024)
    out_ref[3] = nt(inv_ref[0], right)
    for a in range(3):
        at = 1024 + a * 128
        both = got_ref[:, :, at : at + 128].reshape(256, 128).astype(F32).T
        out_ref[a] = both[:64] + both[64:]


def swap(block, pairs):
    return lax.ppermute(block, "leaf", pairs)


def along(block, bits):
    return lax.ppermute(block, "front", [(i, i ^ bits) for i in range(FRONTS)])


def core_pairs():
    return [(i, i ^ 1) for i in range(16)]


def chip_pairs(level):
    pairs = []
    for i in range(16):
        z, core = i // 2, i % 2
        if level == 0:
            to = z ^ 1
        elif level == 1:
            to = z ^ 2
        else:
            to = (6, 7, 4, 5, 2, 3, 0, 1)[z]
        pairs.append((i, 2 * to + core))
    return pairs


def local(rhs_leaf, rhs_top, inv_leaf, inv_top, off_leaf, off_top, idx_leaf, idx_top):
    leaf = lax.axis_index("leaf")
    front = lax.axis_index("front")
    nodes = [jnp.right_shift(16 + leaf, a + 1) for a in range(4)]
    subs = [leaf & (2 ** (a + 1) - 1) for a in range(4)]
    place = nodes + subs + [leaf & 1, front // 4, front % 4]
    place = jnp.stack(place).astype(jnp.int32)
    off_top = jnp.swapaxes(off_top, 1, 2)
    off_leaf = jnp.swapaxes(off_leaf, 1, 2)

    weights = lax.all_to_all(path_weights(place, inv_top, off_top, 3), "front", 0, 0)
    right = rhs_leaf[0].astype(BF)
    one, three, two = [along(right, s) for s in (1, 3, 2)]
    right = jnp.stack([right, one, two, three])
    right = [right] + [along(right, 4 * t) for t in (1, 3, 2)]
    shares = rhs_shares(place, rhs_top)
    piece = jax.ShapeDtypeStruct((64, 1152), BF)
    leaf_x, *sent = pl.pallas_call(
        leaf_solve_kernel,
        out_shape=(jax.ShapeDtypeStruct((64, 256), F32), piece, piece, piece, piece),
        in_specs=[SMEM] + [VMEM] * 7,
        out_specs=(VMEM,) * 5,
        scratch_shapes=[pltpu.VMEM((16, 64, 256), BF), pltpu.VMEM((4, 64, 1024), BF)],
        compiler_params=params(),
    )(place, inv_leaf, right[0], right[1], right[3], right[2], off_leaf, shares)
    got = [sent[0]] + [along(sent[t], 4 * t) for t in (1, 2, 3)]
    piece = jax.ShapeDtypeStruct((16, 1536), F32)
    sent = call(fold_kernel, (piece,) * 4, [SMEM] + [VMEM] * 4, (place, *got))
    got = [sent[0]] + [along(sent[s], s) for s in (1, 2, 3)]
    state = pl.pallas_call(
        leaf_update_kernel,
        out_shape=jax.ShapeDtypeStruct((64, 1024), F32),
        in_specs=[SMEM] + [VMEM] * 5,
        out_specs=VMEM,
        scratch_shapes=[pltpu.VMEM((4, 16, 512), F32)],
        compiler_params=params(),
    )(place, *got, idx_leaf)
    other = swap(state, core_pairs())
    ships = []
    for level in range(3):
        ux, rest = top_solve(state, other, weights, level)
        ux_other = swap(ux, core_pairs())
        state = call(
            functools.partial(update_kernel, level),
            jax.ShapeDtypeStruct(rest.shape, F32),
            [SMEM] + [VMEM] * 4,
            (place, ux, ux_other, rest, idx_top),
        )
        other = swap(state, chip_pairs(level))
        ships.append(
            call(
                ship_kernel,
                jax.ShapeDtypeStruct((16, 16, 128), BF),
                [SMEM, VMEM, VMEM],
                (place, ux, ux_other),
            )
        )
    sent = call(
        root_right_kernel,
        jax.ShapeDtypeStruct((16, 16, 1408), BF),
        [VMEM] * 5,
        (state, other, *ships),
    )
    got = lax.all_to_all(sent, "front", 0, 0)
    ancestors = call(
        root_kernel,
        jax.ShapeDtypeStruct((4, 64, 256), F32),
        [VMEM] * 2,
        (got, inv_top[:1]),
    )
    return (leaf_x[None], ancestors[None])


def solution(mesh):
    placed = (
        P("leaf", "front", None),
        P(None, "front", None),
        P("leaf", "front", None),
        P(None, "front", None),
        P("leaf", None, "front"),
        P(None, None, "front"),
        P("leaf", None),
        P(),
    )
    return jax.shard_map(
        local,
        mesh=mesh,
        in_specs=placed,
        out_specs=(P("leaf", "front", None), P("leaf", None, "front", None)),
        check_vma=False,
    )
```

```python
import functools

import jax
import jax.numpy as jnp
from jax import lax
from jax.experimental import pallas as pl
from jax.experimental.pallas import tpu as pltpu
from jax.sharding import PartitionSpec as P

BF = jnp.bfloat16
F32 = jnp.float32
FRONTS = 16
COLS = 16
WIDTHS = (8, 4, 2, 1)
STARTS = (0, 8, 12, 14)

VMEM = pl.BlockSpec(memory_space=pltpu.VMEM)
SMEM = pl.BlockSpec(memory_space=pltpu.SMEM)
HBM = pl.BlockSpec(memory_space=pltpu.HBM)


def nt(a, b):
    return lax.dot_general(a, b, (((1,), (1,)), ((), ())), preferred_element_type=F32)


def nn(a, b):
    return jnp.dot(a, b, preferred_element_type=F32)


def halves(value):
    high = value.astype(BF)
    low = (value - high.astype(F32)).astype(BF)
    return high, low


def iota(shape, dim):
    return lax.broadcasted_iota(jnp.int32, shape, dim)


def params(mib=16):
    return pltpu.CompilerParams(vmem_limit_bytes=mib * 2**20)


def call(kernel, outs, specs, args, flops=10**8, bytes_accessed=10**6):
    many = isinstance(outs, (tuple, list))
    return pl.pallas_call(
        kernel,
        out_shape=outs,
        in_specs=specs,
        out_specs=tuple(VMEM for _ in outs) if many else VMEM,
        compiler_params=params(),
        cost_estimate=pl.CostEstimate(
            flops=flops, bytes_accessed=bytes_accessed, transcendentals=0
        ),
    )(*args)


def weights_kernel(place, inv_ref, off_ref, out_ref, sems):
    at = pl.ds(pl.multiple_of(place[8] * 32, 32), 32)
    copies = []
    for level in range(3):
        node, to = place[level], level * 64
        for ref, index, to in ((inv_ref, node - 1, to), (off_ref, node - 2, to + 32)):
            copies.append(
                pltpu.make_async_copy(
                    ref.at[index, at, :], out_ref.at[pl.ds(to, 32), :], sems.at[len(copies)]
                )
            )
    for copy in copies:
        copy.start()
    for copy in copies:
        copy.wait()


def path_weights(place, inv_top, off_top):
    return pl.pallas_call(
        weights_kernel,
        out_shape=jax.ShapeDtypeStruct((192, 1024), BF),
        in_specs=[SMEM, HBM, HBM],
        out_specs=HBM,
        scratch_shapes=[pltpu.SemaphoreType.DMA((6,))],
        compiler_params=params(60),
    )(place, inv_top, off_top)


def shares_kernel(place, rhs_ref, out_ref, held, sems):
    copies = [
        pltpu.make_async_copy(rhs_ref.at[place[a] - 1], held.at[a], sems.at[a]) for a in range(4)
    ]
    for copy in copies:
        copy.start()
    for copy in copies:
        copy.wait()
    total = jnp.zeros((256, 256), F32)
    to = iota((256, 256), 0)
    come = iota((256, 256), 1)
    slot = to % 16
    odd = place[9].astype(F32)
    even = 1.0 - odd
    for a in range(4):
        sub = place[4 + a]
        width, start = WIDTHS[a], STARTS[a]
        from_col = (to - slot) + sub * width + (slot - start)
        chosen = (slot >= start) & (slot < start + width) & (come == from_col)
        high, low = halves(held[a])
        high = high.astype(F32)
        low = low.astype(F32)
        stacked = jnp.concatenate([high * even, high * odd, low * even, low * odd], axis=0)
        total = total + nt(jnp.where(chosen, 1.0, 0.0).astype(BF), stacked.astype(BF))
    out_ref[...] = total.astype(BF).reshape(16, 16, 256)


def rhs_shares(place, rhs_top):
    return pl.pallas_call(
        shares_kernel,
        out_shape=jax.ShapeDtypeStruct((16, 16, 256), BF),
        in_specs=[SMEM, HBM],
        out_specs=VMEM,
        scratch_shapes=[pltpu.VMEM((4, 64, 256), F32), pltpu.SemaphoreType.DMA((4,))],
        compiler_params=params(60),
    )(place, rhs_top)


def leaf_solve_kernel(inv_ref, rhs_ref, off_ref, shares_ref, x_ref, out_ref):
    right = rhs_ref[...].reshape(1024, 256)
    x = nn(inv_ref[0], right)
    x_ref[...] = x
    xt = x.T.astype(BF)
    update = nn(xt, off_ref[0])
    out_ref[:, :, :1024] = update.astype(BF).reshape(16, 16, 1024)
    out_ref[:, :, 1024:] = shares_ref[...]


def push(update, idx, count):
    high, low = halves(update)
    both = jnp.concatenate([high, low], axis=0)
    blocks = []
    step = 512
    for a in range(count):
        parts = []
        for t in range(1024 // step):
            hit = iota((step, 1024), 0) + (a * 1024 + t * step) == idx
            got = nt(both, jnp.where(hit, 1.0, 0.0).astype(BF))
            parts.append(got[:16] + got[16:])
        blocks.append(jnp.concatenate(parts, axis=1))
    return blocks


def leaf_update_kernel(place, got_ref, idx_ref, out_ref):
    update = jnp.zeros((16, 1024), F32)
    for s in range(FRONTS):
        update = update + got_ref[s, :, :1024].astype(F32)
    pending = push(update, idx_ref[...], 4)
    high, low = [], []
    for g in range(FRONTS // 2):
        pair = got_ref[2 * g, :, 1024:].astype(F32) + got_ref[2 * g + 1, :, 1024:].astype(F32)
        high.append(pair[:, :128])
        low.append(pair[:, 128:])
    high = jnp.concatenate(high, axis=1).astype(BF)
    low = jnp.concatenate(low, axis=1).astype(BF)
    row = iota((16, 16), 0)
    slot = iota((16, 16), 1)
    for a in range(4):
        width, start = WIDTHS[a], STARTS[a]
        put = (slot >= start) & (slot < start + width)
        put = put & (row == place[4 + a] * width + slot - start)
        put = jnp.where(put, 1.0, 0.0).astype(BF)
        out_ref[a * 16 : (a + 1) * 16, :] = nn(put, high) + nn(put, low) - pending[a]


def solve_kernel(level, own_ref, other_ref, weights_ref, ux_ref, rest_ref, held, sems):
    copies = []
    for part in range(2):
        for half in range(2):
            fronts = pl.ds(half * 8, 8)
            rows = pl.ds(level * 64 + part * 32, 32)
            copies.append(
                pltpu.make_async_copy(
                    weights_ref.at[fronts, rows, :],
                    held.at[part, fronts],
                    sems.at[len(copies)],
                )
            )
    for copy in copies:
        copy.start()
    total = own_ref[...] + other_ref[...]
    rest_ref[...] = total[16:]
    right = total[:16].astype(BF)
    update = jnp.zeros((16, 1024), F32)
    xs = []
    for half in range(2):
        copies[half].wait()
        xs.append(nt(right, held[0, half * 8 : half * 8 + 8].reshape(256, 1024)))
    for half in range(2):
        copies[2 + half].wait()
        off = held[1, half * 8 : half * 8 + 8].reshape(256, 1024)
        update = update + nn(xs[half].astype(BF), off)
        ux_ref[:, 1024 + half * 256 : 1280 + half * 256] = xs[half]
    ux_ref[:, :1024] = update


def top_solve(own, other, weights, level):
    left = own.shape[0] - 16
    return pl.pallas_call(
        functools.partial(solve_kernel, level),
        in_specs=[VMEM, VMEM, HBM],
        out_specs=(VMEM, VMEM),
        out_shape=(jax.ShapeDtypeStruct((16, 1536), F32), jax.ShapeDtypeStruct((left, 1024), F32)),
        scratch_shapes=[pltpu.VMEM((2, 16, 32, 1024), BF), pltpu.SemaphoreType.DMA((4,))],
        compiler_params=params(60 if level == 0 else 16),
    )(own, other, weights)


def update_kernel(level, place, own_ref, other_ref, rest_ref, idx_ref, out_ref):
    update = own_ref[:, :1024] + other_ref[:, :1024]
    count = out_ref.shape[0] // 16
    idx = idx_ref[pl.ds(place[level] - 2, 1), :]
    for a, block in enumerate(push(update, idx, count)):
        out_ref[a * 16 : (a + 1) * 16, :] = rest_ref[a * 16 : (a + 1) * 16, :] - block


def ship_kernel(place, own_ref, other_ref, out_ref):
    first = place[8] == 0
    own = own_ref[:, 1024:]
    other = other_ref[:, 1024:]
    low_core = jnp.where(first, own, other)
    high_core = jnp.where(first, other, own)
    for f in range(FRONTS):
        at = slice(f * 32, (f + 1) * 32)
        value = jnp.concatenate([low_core[:, at], high_core[:, at]], axis=1)
        high = value.astype(BF).astype(F32)
        low = value - high
        out_ref[f] = jnp.concatenate([high, low], axis=1).astype(BF)


def root_right_kernel(own_ref, other_ref, s3_ref, s2_ref, s1_ref, out_ref):
    right = (own_ref[...] + other_ref[...]).astype(BF)
    for f in range(FRONTS):
        out_ref[f, :, :1024] = right
    out_ref[:, :, 1024:1152] = s3_ref[...]
    out_ref[:, :, 1152:1280] = s2_ref[...]
    out_ref[:, :, 1280:] = s1_ref[...]


def root_kernel(got_ref, inv_ref, out_ref):
    right = got_ref[:, :, :1024].reshape(256, 1024)
    out_ref[3] = nt(inv_ref[0], right)
    for a in range(3):
        at = 1024 + a * 128
        both = got_ref[:, :, at : at + 128].reshape(256, 128).astype(F32).T
        out_ref[a] = both[:64] + both[64:]


def swap(block, pairs):
    return lax.ppermute(block, "leaf", pairs)


def core_pairs():
    return [(i, i ^ 1) for i in range(16)]


def chip_pairs(level):
    pairs = []
    for i in range(16):
        z, core = i // 2, i % 2
        if level == 0:
            to = z ^ 1
        elif level == 1:
            to = z ^ 2
        else:
            to = (6, 7, 4, 5, 2, 3, 0, 1)[z]
        pairs.append((i, 2 * to + core))
    return pairs


def local(rhs_leaf, rhs_top, inv_leaf, inv_top, off_leaf, off_top, idx_leaf, idx_top):
    leaf = lax.axis_index("leaf")
    front = lax.axis_index("front")
    nodes = [jnp.right_shift(16 + leaf, a + 1) for a in range(4)]
    subs = [leaf & (2 ** (a + 1) - 1) for a in range(4)]
    place = jnp.stack(nodes + subs + [leaf & 1, front & 1]).astype(jnp.int32)
    off_top = jnp.swapaxes(off_top, 1, 2)
    off_leaf = jnp.swapaxes(off_leaf, 1, 2)

    weights = lax.all_gather(path_weights(place, inv_top, off_top), "front", axis=0)
    right = rhs_leaf[0].astype(BF)
    right = lax.all_to_all(jnp.broadcast_to(right, (FRONTS, *right.shape)), "front", 0, 0)
    shares = rhs_shares(place, rhs_top)
    leaf_x, sent = call(
        leaf_solve_kernel,
        (jax.ShapeDtypeStruct((64, 256), F32), jax.ShapeDtypeStruct((16, 16, 1280), BF)),
        [VMEM] * 4,
        (inv_leaf, right, off_leaf, shares),
    )
    got = lax.all_to_all(sent, "front", 0, 0)
    state = call(
        leaf_update_kernel,
        jax.ShapeDtypeStruct((64, 1024), F32),
        [SMEM, VMEM, VMEM],
        (place, got, idx_leaf),
    )
    other = swap(state, core_pairs())
    ships = []
    for level in range(3):
        ux, rest = top_solve(state, other, weights, level)
        ux_other = swap(ux, core_pairs())
        state = call(
            functools.partial(update_kernel, level),
            jax.ShapeDtypeStruct(rest.shape, F32),
            [SMEM] + [VMEM] * 4,
            (place, ux, ux_other, rest, idx_top),
        )
        other = swap(state, chip_pairs(level))
        ships.append(
            call(
                ship_kernel,
                jax.ShapeDtypeStruct((16, 16, 128), BF),
                [SMEM, VMEM, VMEM],
                (place, ux, ux_other),
            )
        )
    sent = call(
        root_right_kernel,
        jax.ShapeDtypeStruct((16, 16, 1408), BF),
        [VMEM] * 5,
        (state, other, *ships),
    )
    got = lax.all_to_all(sent, "front", 0, 0)
    ancestors = call(
        root_kernel,
        jax.ShapeDtypeStruct((4, 64, 256), F32),
        [VMEM] * 2,
        (got, inv_top[:1]),
    )
    return (leaf_x[None], ancestors[None])


def solution(mesh):
    placed = (
        P("leaf", "front", None),
        P(None, "front", None),
        P("leaf", "front", None),
        P(None, "front", None),
        P("leaf", None, "front"),
        P(None, None, "front"),
        P("leaf", None),
        P(),
    )
    return jax.shard_map(
        local,
        mesh=mesh,
        in_specs=placed,
        out_specs=(P("leaf", "front", None), P("leaf", None, "front", None)),
        check_vma=False,
    )
```

```python
import functools

import jax
import jax.numpy as jnp
from jax import lax
from jax.experimental import pallas as pl
from jax.experimental.pallas import tpu as pltpu
from jax.sharding import PartitionSpec as P

BF = jnp.bfloat16
F32 = jnp.float32
FRONTS = 16
COLS = 16
WIDTHS = (8, 4, 2, 1)
STARTS = (0, 8, 12, 14)

VMEM = pl.BlockSpec(memory_space=pltpu.VMEM)
SMEM = pl.BlockSpec(memory_space=pltpu.SMEM)
HBM = pl.BlockSpec(memory_space=pltpu.HBM)


def nt(a, b):
    return lax.dot_general(a, b, (((1,), (1,)), ((), ())), preferred_element_type=F32)


def nn(a, b):
    return jnp.dot(a, b, preferred_element_type=F32)


def halves(value):
    high = value.astype(BF)
    low = (value - high.astype(F32)).astype(BF)
    return high, low


def iota(shape, dim):
    return lax.broadcasted_iota(jnp.int32, shape, dim)


def params(mib=16):
    return pltpu.CompilerParams(vmem_limit_bytes=mib * 2**20)


def call(kernel, outs, specs, args, flops=10**8, bytes_accessed=10**6):
    many = isinstance(outs, (tuple, list))
    return pl.pallas_call(
        kernel,
        out_shape=outs,
        in_specs=specs,
        out_specs=tuple(VMEM for _ in outs) if many else VMEM,
        compiler_params=params(),
        cost_estimate=pl.CostEstimate(
            flops=flops, bytes_accessed=bytes_accessed, transcendentals=0
        ),
    )(*args)


def first_kernel(place, leaf_ref, rhs_ref, out_ref, held, sems):
    copies = [
        pltpu.make_async_copy(rhs_ref.at[place[a] - 1], held.at[a], sems.at[a]) for a in range(4)
    ]
    for copy in copies:
        copy.start()
    right = leaf_ref[0].astype(BF)
    for f in range(FRONTS):
        out_ref[f, :64, :] = right
    for copy in copies:
        copy.wait()
    total = jnp.zeros((256, 256), F32)
    to = iota((256, 256), 0)
    come = iota((256, 256), 1)
    slot = to % 16
    odd = place[9].astype(F32)
    even = 1.0 - odd
    for a in range(4):
        sub = place[4 + a]
        width, start = WIDTHS[a], STARTS[a]
        from_col = (to - slot) + sub * width + (slot - start)
        chosen = (slot >= start) & (slot < start + width) & (come == from_col)
        high, low = halves(held[a])
        high = high.astype(F32)
        low = low.astype(F32)
        stacked = jnp.concatenate([high * even, high * odd, low * even, low * odd], axis=0)
        total = total + nt(jnp.where(chosen, 1.0, 0.0).astype(BF), stacked.astype(BF))
    out_ref[:, 64:, :] = total.astype(BF).reshape(16, 16, 256)


def first_payload(place, rhs_leaf, rhs_top):
    return pl.pallas_call(
        first_kernel,
        out_shape=jax.ShapeDtypeStruct((FRONTS, 80, 256), BF),
        in_specs=[SMEM, VMEM, HBM],
        out_specs=VMEM,
        scratch_shapes=[pltpu.VMEM((4, 64, 256), F32), pltpu.SemaphoreType.DMA((4,))],
        compiler_params=params(60),
    )(place, rhs_leaf, rhs_top)


def weights_kernel(place, inv_ref, off_ref, *refs):
    outs, sems = refs[:3], refs[3]
    at = pl.ds(pl.multiple_of(place[8] * 32, 32), 32)
    copies = []
    for level, out_ref in enumerate(outs):
        node = place[level]
        for part, (ref, index) in enumerate(((inv_ref, node - 1), (off_ref, node - 2))):
            copies.append(
                pltpu.make_async_copy(
                    ref.at[index, at, :],
                    out_ref.at[pl.ds(part * 32, 32), :],
                    sems.at[len(copies)],
                )
            )
    for copy in copies:
        copy.start()
    for copy in copies:
        copy.wait()


def path_weights(place, inv_top, off_top):
    piece = jax.ShapeDtypeStruct((64, 1024), BF)
    return pl.pallas_call(
        weights_kernel,
        out_shape=(piece,) * 3,
        in_specs=[SMEM, HBM, HBM],
        out_specs=(VMEM,) * 3,
        scratch_shapes=[pltpu.SemaphoreType.DMA((6,))],
        compiler_params=params(60),
    )(place, inv_top, off_top)


def turn(block, dx, dy):
    route = [(i, (i // 4 + dx) % 4 * 4 + (i % 4 + dy) % 4) for i in range(FRONTS)]
    return lax.ppermute(block, "front", route)


def ring(block, axis):
    half = block.shape[0] // 2
    step = (1, 0) if axis == "x" else (0, 1)
    back = tuple(-d for d in step)
    before = turn(block, *step)
    after = turn(block, *back)
    return block, before, after, turn(after[:half], *back), turn(before[half:], *step)


def spread(block, first, second):
    return ring(jnp.concatenate(ring(block, first), axis=0), second)


def leaf_solve_kernel(inv_ref, rhs_ref, off_ref, weights_ref, x_ref, out_ref):
    right = rhs_ref[:, :64, :].reshape(1024, 256)
    x = nn(inv_ref[0], right)
    x_ref[...] = x
    xt = x.T.astype(BF)
    update = nn(xt, off_ref[0])
    out_ref[:, :16, :] = update.astype(BF).reshape(16, 16, 1024)
    for f in range(FRONTS):
        out_ref[f, 16:, :] = weights_ref[...]


def push(update, idx, count):
    high, low = halves(update)
    both = jnp.concatenate([high, low], axis=0)
    blocks = []
    step = 512
    for a in range(count):
        parts = []
        for t in range(1024 // step):
            hit = iota((step, 1024), 0) + (a * 1024 + t * step) == idx
            got = nt(both, jnp.where(hit, 1.0, 0.0).astype(BF))
            parts.append(got[:16] + got[16:])
        blocks.append(jnp.concatenate(parts, axis=1))
    return blocks


def leaf_update_kernel(place, first_ref, got_ref, idx_ref, out_ref):
    update = jnp.zeros((16, 1024), F32)
    for s in range(FRONTS):
        update = update + got_ref[s, :16, :].astype(F32)
    pending = push(update, idx_ref[...], 4)
    high, low = [], []
    for g in range(FRONTS // 2):
        pair = first_ref[2 * g, 64:, :].astype(F32) + first_ref[2 * g + 1, 64:, :].astype(F32)
        high.append(pair[:, :128])
        low.append(pair[:, 128:])
    high = jnp.concatenate(high, axis=1).astype(BF)
    low = jnp.concatenate(low, axis=1).astype(BF)
    row = iota((16, 16), 0)
    slot = iota((16, 16), 1)
    for a in range(4):
        width, start = WIDTHS[a], STARTS[a]
        put = (slot >= start) & (slot < start + width)
        put = put & (row == place[4 + a] * width + slot - start)
        put = jnp.where(put, 1.0, 0.0).astype(BF)
        out_ref[a * 16 : (a + 1) * 16, :] = nn(put, high) + nn(put, low) - pending[a]


def solve_kernel(start, own_ref, other_ref, *refs):
    weights, ux_ref, rest_ref = refs[:-2], refs[-2], refs[-1]
    total = own_ref[...] + other_ref[...]
    rest_ref[...] = total[16:]
    right = total[:16].astype(BF)
    update = jnp.zeros((16, 1024), F32)
    at = 1024
    for ref in weights:
        blocks = ref.shape[0]
        rows = blocks * 32
        x = nt(right, ref[:, start : start + 32, :].reshape(rows, 1024))
        off = ref[:, start + 32 : start + 64, :].reshape(rows, 1024)
        update = update + nn(x.astype(BF), off)
        ux_ref[:, at : at + rows] = x
        at += rows
    ux_ref[:, :1024] = update


def top_solve(own, other, weights, start):
    left = own.shape[0] - 16
    return call(
        functools.partial(solve_kernel, start),
        (jax.ShapeDtypeStruct((16, 1536), F32), jax.ShapeDtypeStruct((left, 1024), F32)),
        [VMEM] * (2 + len(weights)),
        (own, other, *weights),
    )


def update_kernel(level, place, own_ref, other_ref, rest_ref, idx_ref, out_ref):
    update = own_ref[:, :1024] + other_ref[:, :1024]
    count = out_ref.shape[0] // 16
    idx = idx_ref[pl.ds(place[level] - 2, 1), :]
    for a, block in enumerate(push(update, idx, count)):
        out_ref[a * 16 : (a + 1) * 16, :] = rest_ref[a * 16 : (a + 1) * 16, :] - block


def ship_kernel(order, place, own_ref, other_ref, out_ref):
    first = place[8] == 0
    own = own_ref[:, 1024:]
    other = other_ref[:, 1024:]
    low_core = jnp.where(first, own, other)
    high_core = jnp.where(first, other, own)
    for k in range(FRONTS):
        outer, inner = (0, 3, 1, 2)[k // 4], (0, 3, 1, 2)[k % 4]
        if order == "yx":
            to = (place[10] + outer) % 4 * 4 + (place[11] + inner) % 4
        elif order == "xy":
            to = (place[10] + inner) % 4 * 4 + (place[11] + outer) % 4
        else:
            to = k
        at = slice(k * 32, (k + 1) * 32)
        value = jnp.concatenate([low_core[:, at], high_core[:, at]], axis=1)
        high = value.astype(BF).astype(F32)
        low = value - high
        out_ref[to] = jnp.concatenate([high, low], axis=1).astype(BF)


def root_right_kernel(own_ref, other_ref, s3_ref, s2_ref, s1_ref, out_ref):
    right = (own_ref[...] + other_ref[...]).astype(BF)
    for f in range(FRONTS):
        out_ref[f, :, :1024] = right
    out_ref[:, :, 1024:1152] = s3_ref[...]
    out_ref[:, :, 1152:1280] = s2_ref[...]
    out_ref[:, :, 1280:] = s1_ref[...]


def root_kernel(got_ref, inv_ref, out_ref):
    right = got_ref[:, :, :1024].reshape(256, 1024)
    out_ref[3] = nt(inv_ref[0], right)
    for a in range(3):
        at = 1024 + a * 128
        both = got_ref[:, :, at : at + 128].reshape(256, 128).astype(F32).T
        out_ref[a] = both[:64] + both[64:]


def swap(block, pairs):
    return lax.ppermute(block, "leaf", pairs)


def core_pairs():
    return [(i, i ^ 1) for i in range(16)]


def chip_pairs(level):
    pairs = []
    for i in range(16):
        z, core = i // 2, i % 2
        if level == 0:
            to = z ^ 1
        elif level == 1:
            to = z ^ 2
        else:
            to = (6, 7, 4, 5, 2, 3, 0, 1)[z]
        pairs.append((i, 2 * to + core))
    return pairs


def local(rhs_leaf, rhs_top, inv_leaf, inv_top, off_leaf, off_top, idx_leaf, idx_top):
    leaf = lax.axis_index("leaf")
    front = lax.axis_index("front")
    nodes = [jnp.right_shift(16 + leaf, a + 1) for a in range(4)]
    subs = [leaf & (2 ** (a + 1) - 1) for a in range(4)]
    place = nodes + subs + [leaf & 1, front & 1, front // 4, front % 4]
    place = jnp.stack(place).astype(jnp.int32)
    off_top = jnp.swapaxes(off_top, 1, 2)
    off_leaf = jnp.swapaxes(off_leaf, 1, 2)

    first = lax.all_to_all(first_payload(place, rhs_leaf, rhs_top), "front", 0, 0)
    third, second, lowest = path_weights(place, inv_top, off_top)
    leaf_x, sent = call(
        leaf_solve_kernel,
        (jax.ShapeDtypeStruct((64, 256), F32), jax.ShapeDtypeStruct((FRONTS, 80, 1024), BF)),
        [VMEM] * 4,
        (inv_leaf, first, off_leaf, third),
    )
    got = lax.all_to_all(sent, "front", 0, 0)
    weights = [(got,)]
    for block, axes in ((second, "yx"), (lowest, "xy")):
        parts = spread(block, *axes)
        weights.append([part.reshape(-1, 64, 1024) for part in parts])
    state = call(
        leaf_update_kernel,
        jax.ShapeDtypeStruct((64, 1024), F32),
        [SMEM] + [VMEM] * 3,
        (place, first, got, idx_leaf),
    )
    other = swap(state, core_pairs())
    ships = []
    for level in range(3):
        ux, rest = top_solve(state, other, weights[level], 0 if level else 16)
        ux_other = swap(ux, core_pairs())
        state = call(
            functools.partial(update_kernel, level),
            jax.ShapeDtypeStruct(rest.shape, F32),
            [SMEM] + [VMEM] * 4,
            (place, ux, ux_other, rest, idx_top),
        )
        other = swap(state, chip_pairs(level))
        ships.append(
            call(
                functools.partial(ship_kernel, (None, "yx", "xy")[level]),
                jax.ShapeDtypeStruct((16, 16, 128), BF),
                [SMEM, VMEM, VMEM],
                (place, ux, ux_other),
            )
        )
    sent = call(
        root_right_kernel,
        jax.ShapeDtypeStruct((16, 16, 1408), BF),
        [VMEM] * 5,
        (state, other, *ships),
    )
    got = lax.all_to_all(sent, "front", 0, 0)
    ancestors = call(
        root_kernel,
        jax.ShapeDtypeStruct((4, 64, 256), F32),
        [VMEM] * 2,
        (got, inv_top[:1]),
    )
    return (leaf_x[None], ancestors[None])


def solution(mesh):
    placed = (
        P("leaf", "front", None),
        P(None, "front", None),
        P("leaf", "front", None),
        P(None, "front", None),
        P("leaf", None, "front"),
        P(None, None, "front"),
        P("leaf", None),
        P(),
    )
    return jax.shard_map(
        local,
        mesh=mesh,
        in_specs=placed,
        out_specs=(P("leaf", "front", None), P("leaf", None, "front", None)),
        check_vma=False,
    )
```

```python
import functools

import jax
import jax.numpy as jnp
from jax import lax
from jax.experimental import pallas as pl
from jax.experimental.pallas import tpu as pltpu
from jax.sharding import PartitionSpec as P

BF = jnp.bfloat16
F32 = jnp.float32
FRONTS = 16
COLS = 16
WIDTHS = (8, 4, 2, 1)
STARTS = (0, 8, 12, 14)

VMEM = pl.BlockSpec(memory_space=pltpu.VMEM)
SMEM = pl.BlockSpec(memory_space=pltpu.SMEM)
HBM = pl.BlockSpec(memory_space=pltpu.HBM)


def nt(a, b):
    return lax.dot_general(a, b, (((1,), (1,)), ((), ())), preferred_element_type=F32)


def nn(a, b):
    return jnp.dot(a, b, preferred_element_type=F32)


def halves(value):
    high = value.astype(BF)
    low = (value - high.astype(F32)).astype(BF)
    return high, low


def iota(shape, dim):
    return lax.broadcasted_iota(jnp.int32, shape, dim)


def params(mib=12):
    return pltpu.CompilerParams(vmem_limit_bytes=mib * 2**20)


def call(kernel, outs, specs, args, flops=10**8, bytes_accessed=10**6):
    many = isinstance(outs, (tuple, list))
    return pl.pallas_call(
        kernel,
        out_shape=outs,
        in_specs=specs,
        out_specs=tuple(VMEM for _ in outs) if many else VMEM,
        compiler_params=params(),
        cost_estimate=pl.CostEstimate(
            flops=flops, bytes_accessed=bytes_accessed, transcendentals=0
        ),
    )(*args)


def first_kernel(place, leaf_ref, rhs_ref, inv_ref, off_ref, out_ref, *refs):
    pieces, held, sems = refs[:3], refs[3], refs[4]
    copies = [
        pltpu.make_async_copy(rhs_ref.at[place[a] - 1], held.at[a], sems.at[a]) for a in range(4)
    ]
    at = pl.ds(pl.multiple_of(place[8] * 32, 32), 32)
    for level, piece in enumerate(pieces):
        node = place[level]
        for part, (ref, index) in enumerate(((inv_ref, node - 1), (off_ref, node - 2))):
            copies.append(
                pltpu.make_async_copy(
                    ref.at[index, at, :],
                    piece.at[pl.ds(part * 32, 32), :],
                    sems.at[len(copies)],
                )
            )
    for copy in copies:
        copy.start()
    right = leaf_ref[0].astype(BF)
    for f in range(FRONTS):
        out_ref[f, :64, :] = right
    for copy in copies:
        copy.wait()
    total = jnp.zeros((256, 256), F32)
    to = iota((256, 256), 0)
    come = iota((256, 256), 1)
    slot = to % 16
    odd = place[9].astype(F32)
    even = 1.0 - odd
    for a in range(4):
        sub = place[4 + a]
        width, start = WIDTHS[a], STARTS[a]
        from_col = (to - slot) + sub * width + (slot - start)
        chosen = (slot >= start) & (slot < start + width) & (come == from_col)
        high, low = halves(held[a])
        high = high.astype(F32)
        low = low.astype(F32)
        stacked = jnp.concatenate([high * even, high * odd, low * even, low * odd], axis=0)
        total = total + nt(jnp.where(chosen, 1.0, 0.0).astype(BF), stacked.astype(BF))
    out_ref[:, 64:, :] = total.astype(BF).reshape(16, 16, 256)


def first_payload(place, rhs_leaf, rhs_top, inv_top, off_top):
    piece = jax.ShapeDtypeStruct((64, 1024), BF)
    return pl.pallas_call(
        first_kernel,
        out_shape=(jax.ShapeDtypeStruct((FRONTS, 80, 256), BF), piece, piece, piece),
        in_specs=[SMEM, VMEM, HBM, HBM, HBM],
        out_specs=(VMEM,) * 4,
        scratch_shapes=[pltpu.VMEM((4, 64, 256), F32), pltpu.SemaphoreType.DMA((10,))],
        compiler_params=params(60),
    )(place, rhs_leaf, rhs_top, inv_top, off_top)


def stack_kernel(*refs):
    at = 0
    for ref in refs[:-1]:
        rows = ref.shape[0]
        refs[-1][at : at + rows, :] = ref[...]
        at += rows


def stack(parts):
    rows = sum(part.shape[0] for part in parts)
    return call(
        stack_kernel, jax.ShapeDtypeStruct((rows, 1024), BF), [VMEM] * len(parts), tuple(parts)
    )


def turn(block, dx, dy):
    route = [(i, (i // 4 + dx) % 4 * 4 + (i % 4 + dy) % 4) for i in range(FRONTS)]
    return lax.ppermute(block, "front", route)


def step_of(axis):
    return (1, 0) if axis == "x" else (0, 1)


def near(block, axis):
    dx, dy = step_of(axis)
    return turn(block, dx, dy), turn(block, -dx, -dy)


def far(pair, axis):
    dx, dy = step_of(axis)
    before, after = pair
    half = before.shape[0] // 2
    return turn(after[:half], -dx, -dy), turn(before[half:], dx, dy)


def leaf_solve_kernel(inv_ref, rhs_ref, off_ref, x_ref, out_ref):
    right = rhs_ref[:, :64, :].reshape(1024, 256)
    x = nn(inv_ref[0], right)
    x_ref[...] = x
    xt = x.T.astype(BF)
    update = nn(xt, off_ref[0])
    out_ref[...] = update.astype(BF).reshape(16, 16, 1024)


def push(update, idx, count):
    high, low = halves(update)
    both = jnp.concatenate([high, low], axis=0)
    blocks = []
    step = 512
    for a in range(count):
        parts = []
        for t in range(1024 // step):
            hit = iota((step, 1024), 0) + (a * 1024 + t * step) == idx
            got = nt(both, jnp.where(hit, 1.0, 0.0).astype(BF))
            parts.append(got[:16] + got[16:])
        blocks.append(jnp.concatenate(parts, axis=1))
    return blocks


def leaf_update_kernel(place, first_ref, got_ref, idx_ref, out_ref):
    update = jnp.zeros((16, 1024), F32)
    for s in range(FRONTS):
        update = update + got_ref[s].astype(F32)
    pending = push(update, idx_ref[...], 4)
    high, low = [], []
    for g in range(FRONTS // 2):
        pair = first_ref[2 * g, 64:, :].astype(F32) + first_ref[2 * g + 1, 64:, :].astype(F32)
        high.append(pair[:, :128])
        low.append(pair[:, 128:])
    high = jnp.concatenate(high, axis=1).astype(BF)
    low = jnp.concatenate(low, axis=1).astype(BF)
    row = iota((16, 16), 0)
    slot = iota((16, 16), 1)
    for a in range(4):
        width, start = WIDTHS[a], STARTS[a]
        put = (slot >= start) & (slot < start + width)
        put = put & (row == place[4 + a] * width + slot - start)
        put = jnp.where(put, 1.0, 0.0).astype(BF)
        out_ref[a * 16 : (a + 1) * 16, :] = nn(put, high) + nn(put, low) - pending[a]


def solve_kernel(own_ref, other_ref, *refs):
    weights, ux_ref, rest_ref = refs[:-2], refs[-2], refs[-1]
    total = own_ref[...] + other_ref[...]
    rest_ref[...] = total[16:]
    right = total[:16].astype(BF)
    update = jnp.zeros((16, 1024), F32)
    at = 1024
    for ref in weights:
        blocks = ref.shape[0]
        rows = blocks * 32
        x = nt(right, ref[:, :32, :].reshape(rows, 1024))
        off = ref[:, 32:, :].reshape(rows, 1024)
        update = update + nn(x.astype(BF), off)
        ux_ref[:, at : at + rows] = x
        at += rows
    ux_ref[:, :1024] = update


def top_solve(own, other, weights):
    left = own.shape[0] - 16
    return call(
        solve_kernel,
        (jax.ShapeDtypeStruct((16, 1536), F32), jax.ShapeDtypeStruct((left, 1024), F32)),
        [VMEM] * (2 + len(weights)),
        (own, other, *weights),
    )


def update_kernel(level, place, own_ref, other_ref, rest_ref, idx_ref, out_ref):
    update = own_ref[:, :1024] + other_ref[:, :1024]
    count = out_ref.shape[0] // 16
    idx = idx_ref[pl.ds(place[level] - 2, 1), :]
    for a, block in enumerate(push(update, idx, count)):
        out_ref[a * 16 : (a + 1) * 16, :] = rest_ref[a * 16 : (a + 1) * 16, :] - block


def ship_kernel(order, place, own_ref, other_ref, out_ref):
    first = place[8] == 0
    own = own_ref[:, 1024:]
    other = other_ref[:, 1024:]
    low_core = jnp.where(first, own, other)
    high_core = jnp.where(first, other, own)
    for k in range(FRONTS):
        outer, inner = (0, 3, 1, 2)[k // 4], (0, 3, 1, 2)[k % 4]
        if order == "yx":
            to = (place[10] + outer) % 4 * 4 + (place[11] + inner) % 4
        else:
            to = (place[10] + inner) % 4 * 4 + (place[11] + outer) % 4
        at = slice(k * 32, (k + 1) * 32)
        value = jnp.concatenate([low_core[:, at], high_core[:, at]], axis=1)
        high = value.astype(BF).astype(F32)
        low = value - high
        out_ref[to] = jnp.concatenate([high, low], axis=1).astype(BF)


def root_right_kernel(own_ref, other_ref, s3_ref, s2_ref, s1_ref, out_ref):
    right = (own_ref[...] + other_ref[...]).astype(BF)
    for f in range(FRONTS):
        out_ref[f, :, :1024] = right
    out_ref[:, :, 1024:1152] = s3_ref[...]
    out_ref[:, :, 1152:1280] = s2_ref[...]
    out_ref[:, :, 1280:] = s1_ref[...]


def root_kernel(got_ref, inv_ref, out_ref):
    right = got_ref[:, :, :1024].reshape(256, 1024)
    out_ref[3] = nt(inv_ref[0], right)
    for a in range(3):
        at = 1024 + a * 128
        both = got_ref[:, :, at : at + 128].reshape(256, 128).astype(F32).T
        out_ref[a] = both[:64] + both[64:]


def swap(block, pairs):
    return lax.ppermute(block, "leaf", pairs)


def core_pairs():
    return [(i, i ^ 1) for i in range(16)]


def chip_pairs(level):
    pairs = []
    for i in range(16):
        z, core = i // 2, i % 2
        if level == 0:
            to = z ^ 1
        elif level == 1:
            to = z ^ 2
        else:
            to = (6, 7, 4, 5, 2, 3, 0, 1)[z]
        pairs.append((i, 2 * to + core))
    return pairs


def local(rhs_leaf, rhs_top, inv_leaf, inv_top, off_leaf, off_top, idx_leaf, idx_top):
    leaf = lax.axis_index("leaf")
    front = lax.axis_index("front")
    nodes = [jnp.right_shift(16 + leaf, a + 1) for a in range(4)]
    subs = [leaf & (2 ** (a + 1) - 1) for a in range(4)]
    place = nodes + subs + [leaf & 1, front & 1, front // 4, front % 4]
    place = jnp.stack(place).astype(jnp.int32)
    off_top = jnp.swapaxes(off_top, 1, 2)
    off_leaf = jnp.swapaxes(off_leaf, 1, 2)

    sent, third, second, lowest = first_payload(place, rhs_leaf, rhs_top, inv_top, off_top)
    first = lax.all_to_all(sent, "front", 0, 0)
    third_near, second_near, lowest_near = near(third, "y"), near(second, "x"), near(lowest, "y")
    third = (third, *third_near, *far(third_near, "y"))
    second = (second, *second_near, *far(second_near, "x"))
    lowest = (lowest, *lowest_near, *far(lowest_near, "y"))
    leaf_x, sent = call(
        leaf_solve_kernel,
        (jax.ShapeDtypeStruct((64, 256), F32), jax.ShapeDtypeStruct((FRONTS, 16, 1024), BF)),
        [VMEM] * 3,
        (inv_leaf, first, off_leaf),
    )
    sent, third, second, lowest = lax.optimization_barrier((sent, third, second, lowest))
    got = lax.all_to_all(sent, "front", 0, 0)
    third, second = stack(third), stack(second)
    third_near, second_near = near(third, "x"), near(second, "y")
    state = call(
        leaf_update_kernel,
        jax.ShapeDtypeStruct((64, 1024), F32),
        [SMEM] + [VMEM] * 3,
        (place, first, got, idx_leaf),
    )
    state, third_near, second_near = lax.optimization_barrier((state, third_near, second_near))
    third_far, second_far = far(third_near, "x"), far(second_near, "y")
    other = swap(state, core_pairs())
    ships = []
    for level in range(3):
        if level == 0:
            parts = (third, *third_near, *third_far)
        elif level == 1:
            parts = (second, *second_near, *second_far)
        else:
            parts = (lowest, *lowest_near, *lowest_far)
        ux, rest = top_solve(state, other, [part.reshape(-1, 64, 1024) for part in parts])
        if level == 0:
            ux, lowest, second_far = lax.optimization_barrier((ux, lowest, second_far))
            lowest = stack(lowest)
            lowest_near = near(lowest, "x")
        ux_other = swap(ux, core_pairs())
        state = call(
            functools.partial(update_kernel, level),
            jax.ShapeDtypeStruct(rest.shape, F32),
            [SMEM] + [VMEM] * 4,
            (place, ux, ux_other, rest, idx_top),
        )
        other = swap(state, chip_pairs(level))
        if level == 0:
            other, lowest_near = lax.optimization_barrier((other, lowest_near))
            lowest_far = far(lowest_near, "x")
        ships.append(
            call(
                functools.partial(ship_kernel, ("yx", "xy", "yx")[level]),
                jax.ShapeDtypeStruct((16, 16, 128), BF),
                [SMEM, VMEM, VMEM],
                (place, ux, ux_other),
            )
        )
    sent = call(
        root_right_kernel,
        jax.ShapeDtypeStruct((16, 16, 1408), BF),
        [VMEM] * 5,
        (state, other, *ships),
    )
    got = lax.all_to_all(sent, "front", 0, 0)
    ancestors = call(
        root_kernel,
        jax.ShapeDtypeStruct((4, 64, 256), F32),
        [VMEM] * 2,
        (got, inv_top[:1]),
    )
    return (leaf_x[None], ancestors[None])


def solution(mesh):
    placed = (
        P("leaf", "front", None),
        P(None, "front", None),
        P("leaf", "front", None),
        P(None, "front", None),
        P("leaf", None, "front"),
        P(None, None, "front"),
        P("leaf", None),
        P(),
    )
    return jax.shard_map(
        local,
        mesh=mesh,
        in_specs=placed,
        out_specs=(P("leaf", "front", None), P("leaf", None, "front", None)),
        check_vma=False,
    )
```

```python
import functools

import jax
import jax.numpy as jnp
from jax import lax
from jax.experimental import pallas as pl
from jax.experimental.pallas import tpu as pltpu
from jax.sharding import PartitionSpec as P

BF = jnp.bfloat16
F32 = jnp.float32
FRONTS = 16
COLS = 16
WIDTHS = (8, 4, 2, 1)
STARTS = (0, 8, 12, 14)

VMEM = pl.BlockSpec(memory_space=pltpu.VMEM)
SMEM = pl.BlockSpec(memory_space=pltpu.SMEM)
HBM = pl.BlockSpec(memory_space=pltpu.HBM)


def nt(a, b):
    return lax.dot_general(a, b, (((1,), (1,)), ((), ())), preferred_element_type=F32)


def nn(a, b):
    return jnp.dot(a, b, preferred_element_type=F32)


def halves(value):
    high = value.astype(BF)
    low = (value - high.astype(F32)).astype(BF)
    return high, low


def iota(shape, dim):
    return lax.broadcasted_iota(jnp.int32, shape, dim)


def params(mib=12):
    return pltpu.CompilerParams(vmem_limit_bytes=mib * 2**20)


def call(kernel, outs, specs, args, flops=10**8, bytes_accessed=10**6):
    many = isinstance(outs, (tuple, list))
    return pl.pallas_call(
        kernel,
        out_shape=outs,
        in_specs=specs,
        out_specs=tuple(VMEM for _ in outs) if many else VMEM,
        compiler_params=params(),
        cost_estimate=pl.CostEstimate(
            flops=flops, bytes_accessed=bytes_accessed, transcendentals=0
        ),
    )(*args)


def first_kernel(place, leaf_ref, rhs_ref, inv_ref, off_ref, out_ref, *refs):
    ends_ref, middle_ref, held, sems = refs
    copies = [
        pltpu.make_async_copy(rhs_ref.at[place[a] - 1], held.at[a], sems.at[a]) for a in range(4)
    ]
    at = pl.ds(pl.multiple_of(place[8] * 32, 32), 32)
    for level, (piece, start) in enumerate(((ends_ref, 0), (middle_ref, 0), (ends_ref, 64))):
        node = place[level]
        for part, (ref, index) in enumerate(((inv_ref, node - 1), (off_ref, node - 2))):
            copies.append(
                pltpu.make_async_copy(
                    ref.at[index, at, :],
                    piece.at[pl.ds(start + part * 32, 32), :],
                    sems.at[len(copies)],
                )
            )
    for copy in copies:
        copy.start()
    right = leaf_ref[0].astype(BF)
    for f in range(FRONTS):
        out_ref[f, :64, :] = right
    for copy in copies:
        copy.wait()
    total = jnp.zeros((256, 256), F32)
    to = iota((256, 256), 0)
    come = iota((256, 256), 1)
    slot = to % 16
    odd = place[9].astype(F32)
    even = 1.0 - odd
    for a in range(4):
        sub = place[4 + a]
        width, start = WIDTHS[a], STARTS[a]
        from_col = (to - slot) + sub * width + (slot - start)
        chosen = (slot >= start) & (slot < start + width) & (come == from_col)
        high, low = halves(held[a])
        high = high.astype(F32)
        low = low.astype(F32)
        stacked = jnp.concatenate([high * even, high * odd, low * even, low * odd], axis=0)
        total = total + nt(jnp.where(chosen, 1.0, 0.0).astype(BF), stacked.astype(BF))
    out_ref[:, 64:, :] = total.astype(BF).reshape(16, 16, 256)


def first_payload(place, rhs_leaf, rhs_top, inv_top, off_top):
    return pl.pallas_call(
        first_kernel,
        out_shape=(
            jax.ShapeDtypeStruct((FRONTS, 80, 256), BF),
            jax.ShapeDtypeStruct((128, 1024), BF),
            jax.ShapeDtypeStruct((64, 1024), BF),
        ),
        in_specs=[SMEM, VMEM, HBM, HBM, HBM],
        out_specs=(VMEM,) * 3,
        scratch_shapes=[pltpu.VMEM((4, 64, 256), F32), pltpu.SemaphoreType.DMA((10,))],
        compiler_params=params(60),
    )(place, rhs_leaf, rhs_top, inv_top, off_top)


def stack_kernel(start, *refs):
    for k, ref in enumerate(refs[:-1]):
        refs[-1][k * 64 : (k + 1) * 64, :] = ref[start : start + 64, :]


def stack(parts, start):
    rows = 64 * len(parts)
    return call(
        functools.partial(stack_kernel, start),
        jax.ShapeDtypeStruct((rows, 1024), BF),
        [VMEM] * len(parts),
        tuple(parts),
    )


def turn(block, dx, dy):
    route = [(i, (i // 4 + dx) % 4 * 4 + (i % 4 + dy) % 4) for i in range(FRONTS)]
    return lax.ppermute(block, "front", route)


def step_of(axis):
    return (1, 0) if axis == "x" else (0, 1)


def near(block, axis):
    dx, dy = step_of(axis)
    return turn(block, dx, dy), turn(block, -dx, -dy)


def around(block, axis):
    dx, dy = step_of(axis)
    opposite = turn(block, 2 * dx, 2 * dy)
    return (block, *near(block, axis), opposite)


def far(pair, axis):
    dx, dy = step_of(axis)
    before, after = pair
    half = before.shape[0] // 2
    return turn(after[:half], -dx, -dy), turn(before[half:], dx, dy)


def leaf_solve_kernel(inv_ref, rhs_ref, off_ref, x_ref, out_ref):
    right = rhs_ref[:, :64, :].reshape(1024, 256)
    x = nn(inv_ref[0], right)
    x_ref[...] = x
    xt = x.T.astype(BF)
    update = nn(xt, off_ref[0])
    out_ref[...] = update.astype(BF).reshape(16, 16, 1024)


def push(update, idx, count):
    high, low = halves(update)
    both = jnp.concatenate([high, low], axis=0)
    blocks = []
    step = 512
    for a in range(count):
        parts = []
        for t in range(1024 // step):
            hit = iota((step, 1024), 0) + (a * 1024 + t * step) == idx
            got = nt(both, jnp.where(hit, 1.0, 0.0).astype(BF))
            parts.append(got[:16] + got[16:])
        blocks.append(jnp.concatenate(parts, axis=1))
    return blocks


def leaf_update_kernel(place, first_ref, got_ref, idx_ref, out_ref):
    update = jnp.zeros((16, 1024), F32)
    for s in range(FRONTS):
        update = update + got_ref[s].astype(F32)
    pending = push(update, idx_ref[...], 4)
    high, low = [], []
    for g in range(FRONTS // 2):
        pair = first_ref[2 * g, 64:, :].astype(F32) + first_ref[2 * g + 1, 64:, :].astype(F32)
        high.append(pair[:, :128])
        low.append(pair[:, 128:])
    high = jnp.concatenate(high, axis=1).astype(BF)
    low = jnp.concatenate(low, axis=1).astype(BF)
    row = iota((16, 16), 0)
    slot = iota((16, 16), 1)
    for a in range(4):
        width, start = WIDTHS[a], STARTS[a]
        put = (slot >= start) & (slot < start + width)
        put = put & (row == place[4 + a] * width + slot - start)
        put = jnp.where(put, 1.0, 0.0).astype(BF)
        out_ref[a * 16 : (a + 1) * 16, :] = nn(put, high) + nn(put, low) - pending[a]


def solve_kernel(own_ref, other_ref, *refs):
    weights, ux_ref, rest_ref = refs[:-2], refs[-2], refs[-1]
    total = own_ref[...] + other_ref[...]
    rest_ref[...] = total[16:]
    right = total[:16].astype(BF)
    update = jnp.zeros((16, 1024), F32)
    at = 1024
    for ref in weights:
        blocks = ref.shape[0]
        rows = blocks * 32
        x = nt(right, ref[:, :32, :].reshape(rows, 1024))
        off = ref[:, 32:, :].reshape(rows, 1024)
        update = update + nn(x.astype(BF), off)
        ux_ref[:, at : at + rows] = x
        at += rows
    ux_ref[:, :1024] = update


def top_solve(own, other, weights):
    left = own.shape[0] - 16
    return call(
        solve_kernel,
        (jax.ShapeDtypeStruct((16, 1536), F32), jax.ShapeDtypeStruct((left, 1024), F32)),
        [VMEM] * (2 + len(weights)),
        (own, other, *weights),
    )


def update_kernel(level, place, own_ref, other_ref, rest_ref, idx_ref, out_ref):
    update = own_ref[:, :1024] + other_ref[:, :1024]
    count = out_ref.shape[0] // 16
    idx = idx_ref[pl.ds(place[level] - 2, 1), :]
    for a, block in enumerate(push(update, idx, count)):
        out_ref[a * 16 : (a + 1) * 16, :] = rest_ref[a * 16 : (a + 1) * 16, :] - block


def ship_kernel(order, place, own_ref, other_ref, out_ref):
    first = place[8] == 0
    own = own_ref[:, 1024:]
    other = other_ref[:, 1024:]
    low_core = jnp.where(first, own, other)
    high_core = jnp.where(first, other, own)
    for k in range(FRONTS):
        outer, inner = (0, 3, 1, 2)[k // 4], (0, 3, 1, 2)[k % 4]
        if order == "yx":
            to = (place[10] + outer) % 4 * 4 + (place[11] + inner) % 4
        else:
            to = (place[10] + inner) % 4 * 4 + (place[11] + outer) % 4
        at = slice(k * 32, (k + 1) * 32)
        value = jnp.concatenate([low_core[:, at], high_core[:, at]], axis=1)
        high = value.astype(BF).astype(F32)
        low = value - high
        out_ref[to] = jnp.concatenate([high, low], axis=1).astype(BF)


def root_right_kernel(own_ref, other_ref, s3_ref, s2_ref, s1_ref, out_ref):
    right = (own_ref[...] + other_ref[...]).astype(BF)
    for f in range(FRONTS):
        out_ref[f, :, :1024] = right
    out_ref[:, :, 1024:1152] = s3_ref[...]
    out_ref[:, :, 1152:1280] = s2_ref[...]
    out_ref[:, :, 1280:] = s1_ref[...]


def root_kernel(got_ref, inv_ref, out_ref):
    right = got_ref[:, :, :1024].reshape(256, 1024)
    out_ref[3] = nt(inv_ref[0], right)
    for a in range(3):
        at = 1024 + a * 128
        both = got_ref[:, :, at : at + 128].reshape(256, 128).astype(F32).T
        out_ref[a] = both[:64] + both[64:]


def swap(block, pairs):
    return lax.ppermute(block, "leaf", pairs)


def core_pairs():
    return [(i, i ^ 1) for i in range(16)]


def chip_pairs(level):
    pairs = []
    for i in range(16):
        z, core = i // 2, i % 2
        if level == 0:
            to = z ^ 1
        elif level == 1:
            to = z ^ 2
        else:
            to = (6, 7, 4, 5, 2, 3, 0, 1)[z]
        pairs.append((i, 2 * to + core))
    return pairs


def local(rhs_leaf, rhs_top, inv_leaf, inv_top, off_leaf, off_top, idx_leaf, idx_top):
    leaf = lax.axis_index("leaf")
    front = lax.axis_index("front")
    nodes = [jnp.right_shift(16 + leaf, a + 1) for a in range(4)]
    subs = [leaf & (2 ** (a + 1) - 1) for a in range(4)]
    place = nodes + subs + [leaf & 1, front & 1, front // 4, front % 4]
    place = jnp.stack(place).astype(jnp.int32)
    off_top = jnp.swapaxes(off_top, 1, 2)
    off_leaf = jnp.swapaxes(off_leaf, 1, 2)

    sent, ends, middle = first_payload(place, rhs_leaf, rhs_top, inv_top, off_top)
    first = lax.all_to_all(sent, "front", 0, 0)
    ends, middle = around(ends, "y"), around(middle, "x")
    leaf_x, sent = call(
        leaf_solve_kernel,
        (jax.ShapeDtypeStruct((64, 256), F32), jax.ShapeDtypeStruct((FRONTS, 16, 1024), BF)),
        [VMEM] * 3,
        (inv_leaf, first, off_leaf),
    )
    sent, ends, middle = lax.optimization_barrier((sent, ends, middle))
    got = lax.all_to_all(sent, "front", 0, 0)
    third, second, lowest = stack(ends, 0), stack(middle, 0), stack(ends, 64)
    third_near, second_near = near(third, "x"), near(second, "y")
    third_far, second_far = far(third_near, "x"), far(second_near, "y")
    got, third_far, second_far, lowest = lax.optimization_barrier(
        (got, third_far, second_far, lowest)
    )
    lowest_near = near(lowest, "x")
    state = call(
        leaf_update_kernel,
        jax.ShapeDtypeStruct((64, 1024), F32),
        [SMEM] + [VMEM] * 3,
        (place, first, got, idx_leaf),
    )
    other = swap(state, core_pairs())
    ships = []
    for level in range(3):
        if level == 0:
            parts = (third, *third_near, *third_far)
        elif level == 1:
            parts = (second, *second_near, *second_far)
        else:
            parts = (lowest, *lowest_near, *lowest_far)
        ux, rest = top_solve(state, other, [part.reshape(-1, 64, 1024) for part in parts])
        ux_other = swap(ux, core_pairs())
        state = call(
            functools.partial(update_kernel, level),
            jax.ShapeDtypeStruct(rest.shape, F32),
            [SMEM] + [VMEM] * 4,
            (place, ux, ux_other, rest, idx_top),
        )
        other = swap(state, chip_pairs(level))
        if level == 0:
            other, lowest_near = lax.optimization_barrier((other, lowest_near))
            lowest_far = far(lowest_near, "x")
        ships.append(
            call(
                functools.partial(ship_kernel, ("yx", "xy", "yx")[level]),
                jax.ShapeDtypeStruct((16, 16, 128), BF),
                [SMEM, VMEM, VMEM],
                (place, ux, ux_other),
            )
        )
    sent = call(
        root_right_kernel,
        jax.ShapeDtypeStruct((16, 16, 1408), BF),
        [VMEM] * 5,
        (state, other, *ships),
    )
    got = lax.all_to_all(sent, "front", 0, 0)
    ancestors = call(
        root_kernel,
        jax.ShapeDtypeStruct((4, 64, 256), F32),
        [VMEM] * 2,
        (got, inv_top[:1]),
    )
    return (leaf_x[None], ancestors[None])


def solution(mesh):
    placed = (
        P("leaf", "front", None),
        P(None, "front", None),
        P("leaf", "front", None),
        P(None, "front", None),
        P("leaf", None, "front"),
        P(None, None, "front"),
        P("leaf", None),
        P(),
    )
    return jax.shard_map(
        local,
        mesh=mesh,
        in_specs=placed,
        out_specs=(P("leaf", "front", None), P("leaf", None, "front", None)),
        check_vma=False,
    )
```

```python
import functools

import jax
import jax.numpy as jnp
from jax import lax
from jax.experimental import pallas as pl
from jax.experimental.pallas import tpu as pltpu
from jax.sharding import PartitionSpec as P

BF = jnp.bfloat16
F32 = jnp.float32
FRONTS = 16
COLS = 16
WIDTHS = (8, 4, 2, 1)
STARTS = (0, 8, 12, 14)

VMEM = pl.BlockSpec(memory_space=pltpu.VMEM)
SMEM = pl.BlockSpec(memory_space=pltpu.SMEM)
HBM = pl.BlockSpec(memory_space=pltpu.HBM)


def nt(a, b):
    return lax.dot_general(a, b, (((1,), (1,)), ((), ())), preferred_element_type=F32)


def nn(a, b):
    return jnp.dot(a, b, preferred_element_type=F32)


def halves(value):
    high = value.astype(BF)
    low = (value - high.astype(F32)).astype(BF)
    return high, low


def iota(shape, dim):
    return lax.broadcasted_iota(jnp.int32, shape, dim)


def params(mib=12):
    return pltpu.CompilerParams(vmem_limit_bytes=mib * 2**20)


def call(kernel, outs, specs, args, flops=10**8, bytes_accessed=10**6):
    many = isinstance(outs, (tuple, list))
    return pl.pallas_call(
        kernel,
        out_shape=outs,
        in_specs=specs,
        out_specs=tuple(VMEM for _ in outs) if many else VMEM,
        compiler_params=params(),
        cost_estimate=pl.CostEstimate(
            flops=flops, bytes_accessed=bytes_accessed, transcendentals=0
        ),
    )(*args)


def first_kernel(place, leaf_ref, rhs_ref, inv_ref, off_ref, out_ref, *refs):
    third_ref, pair_ref, held, sems = refs
    copies = [
        pltpu.make_async_copy(rhs_ref.at[place[a] - 1], held.at[a], sems.at[a]) for a in range(4)
    ]
    at = pl.ds(pl.multiple_of(place[8] * 32, 32), 32)
    for level, (piece, start) in enumerate(((third_ref, 0), (pair_ref, 0), (pair_ref, 64))):
        node = place[level]
        for part, (ref, index) in enumerate(((inv_ref, node - 1), (off_ref, node - 2))):
            copies.append(
                pltpu.make_async_copy(
                    ref.at[index, at, :],
                    piece.at[pl.ds(start + part * 32, 32), :],
                    sems.at[len(copies)],
                )
            )
    for copy in copies:
        copy.start()
    right = leaf_ref[0].astype(BF)
    for f in range(FRONTS):
        out_ref[f, :64, :] = right
    for copy in copies:
        copy.wait()
    total = jnp.zeros((256, 256), F32)
    to = iota((256, 256), 0)
    come = iota((256, 256), 1)
    slot = to % 16
    odd = place[9].astype(F32)
    even = 1.0 - odd
    for a in range(4):
        sub = place[4 + a]
        width, start = WIDTHS[a], STARTS[a]
        from_col = (to - slot) + sub * width + (slot - start)
        chosen = (slot >= start) & (slot < start + width) & (come == from_col)
        high, low = halves(held[a])
        high = high.astype(F32)
        low = low.astype(F32)
        stacked = jnp.concatenate([high * even, high * odd, low * even, low * odd], axis=0)
        total = total + nt(jnp.where(chosen, 1.0, 0.0).astype(BF), stacked.astype(BF))
    out_ref[:, 64:, :] = total.astype(BF).reshape(16, 16, 256)


def first_payload(place, rhs_leaf, rhs_top, inv_top, off_top):
    return pl.pallas_call(
        first_kernel,
        out_shape=(
            jax.ShapeDtypeStruct((FRONTS, 80, 256), BF),
            jax.ShapeDtypeStruct((64, 1024), BF),
            jax.ShapeDtypeStruct((128, 1024), BF),
        ),
        in_specs=[SMEM, VMEM, HBM, HBM, HBM],
        out_specs=(VMEM,) * 3,
        scratch_shapes=[pltpu.VMEM((4, 64, 256), F32), pltpu.SemaphoreType.DMA((10,))],
        compiler_params=params(60),
    )(place, rhs_leaf, rhs_top, inv_top, off_top)


def stack_kernel(own_ref, before_ref, after_ref, second_ref, lowest_ref, *outs):
    for level, (opposite_ref, out_ref) in enumerate(zip((second_ref, lowest_ref), outs)):
        at = slice(level * 64, (level + 1) * 64)
        for k, ref in enumerate((own_ref, before_ref, after_ref)):
            out_ref[k * 64 : (k + 1) * 64, :] = ref[at, :]
        out_ref[192:, :] = opposite_ref[...]


def stack(parts):
    piece = jax.ShapeDtypeStruct((256, 1024), BF)
    return call(stack_kernel, (piece, piece), [VMEM] * 5, parts)


def turn(block, dx, dy):
    route = [(i, (i // 4 + dx) % 4 * 4 + (i % 4 + dy) % 4) for i in range(FRONTS)]
    return lax.ppermute(block, "front", route)


def step_of(axis):
    return (1, 0) if axis == "x" else (0, 1)


def near(block, axis):
    dx, dy = step_of(axis)
    return turn(block, dx, dy), turn(block, -dx, -dy)


def far(pair, axis):
    dx, dy = step_of(axis)
    before, after = pair
    half = before.shape[0] // 2
    return turn(after[:half], -dx, -dy), turn(before[half:], dx, dy)


def leaf_solve_kernel(inv_ref, rhs_ref, off_ref, third_ref, x_ref, out_ref):
    right = rhs_ref[:, :64, :].reshape(1024, 256)
    x = nn(inv_ref[0], right)
    x_ref[...] = x
    xt = x.T.astype(BF)
    update = nn(xt, off_ref[0])
    out_ref[:, :16, :] = update.astype(BF).reshape(16, 16, 1024)
    for f in range(FRONTS):
        out_ref[f, 16:, :] = third_ref[...]


def push(update, idx, count):
    high, low = halves(update)
    both = jnp.concatenate([high, low], axis=0)
    blocks = []
    step = 512
    for a in range(count):
        parts = []
        for t in range(1024 // step):
            hit = iota((step, 1024), 0) + (a * 1024 + t * step) == idx
            got = nt(both, jnp.where(hit, 1.0, 0.0).astype(BF))
            parts.append(got[:16] + got[16:])
        blocks.append(jnp.concatenate(parts, axis=1))
    return blocks


def leaf_update_kernel(place, first_ref, got_ref, idx_ref, out_ref):
    update = jnp.zeros((16, 1024), F32)
    for s in range(FRONTS):
        update = update + got_ref[s, :16, :].astype(F32)
    pending = push(update, idx_ref[...], 4)
    high, low = [], []
    for g in range(FRONTS // 2):
        pair = first_ref[2 * g, 64:, :].astype(F32) + first_ref[2 * g + 1, 64:, :].astype(F32)
        high.append(pair[:, :128])
        low.append(pair[:, 128:])
    high = jnp.concatenate(high, axis=1).astype(BF)
    low = jnp.concatenate(low, axis=1).astype(BF)
    row = iota((16, 16), 0)
    slot = iota((16, 16), 1)
    for a in range(4):
        width, start = WIDTHS[a], STARTS[a]
        put = (slot >= start) & (slot < start + width)
        put = put & (row == place[4 + a] * width + slot - start)
        put = jnp.where(put, 1.0, 0.0).astype(BF)
        out_ref[a * 16 : (a + 1) * 16, :] = nn(put, high) + nn(put, low) - pending[a]


def solve_kernel(start, own_ref, other_ref, *refs):
    weights, ux_ref, rest_ref = refs[:-2], refs[-2], refs[-1]
    total = own_ref[...] + other_ref[...]
    rest_ref[...] = total[16:]
    right = total[:16].astype(BF)
    update = jnp.zeros((16, 1024), F32)
    at = 1024
    for ref in weights:
        blocks = ref.shape[0]
        rows = blocks * 32
        x = nt(right, ref[:, start : start + 32, :].reshape(rows, 1024))
        off = ref[:, start + 32 : start + 64, :].reshape(rows, 1024)
        update = update + nn(x.astype(BF), off)
        ux_ref[:, at : at + rows] = x
        at += rows
    ux_ref[:, :1024] = update


def top_solve(own, other, weights):
    left = own.shape[0] - 16
    start = weights[0].shape[1] - 64
    return call(
        functools.partial(solve_kernel, start),
        (jax.ShapeDtypeStruct((16, 1536), F32), jax.ShapeDtypeStruct((left, 1024), F32)),
        [VMEM] * (2 + len(weights)),
        (own, other, *weights),
    )


def update_kernel(level, place, own_ref, other_ref, rest_ref, idx_ref, out_ref):
    update = own_ref[:, :1024] + other_ref[:, :1024]
    count = out_ref.shape[0] // 16
    idx = idx_ref[pl.ds(place[level] - 2, 1), :]
    for a, block in enumerate(push(update, idx, count)):
        out_ref[a * 16 : (a + 1) * 16, :] = rest_ref[a * 16 : (a + 1) * 16, :] - block


def ship_kernel(turned, place, own_ref, other_ref, out_ref):
    first = place[8] == 0
    own = own_ref[:, 1024:]
    other = other_ref[:, 1024:]
    low_core = jnp.where(first, own, other)
    high_core = jnp.where(first, other, own)
    for k in range(FRONTS):
        outer, inner = (0, 3, 1, 2)[k // 4], (0, 3, 1, 2)[k % 4]
        to = k
        if turned:
            to = (place[10] + outer) % 4 * 4 + (place[11] + inner) % 4
        at = slice(k * 32, (k + 1) * 32)
        value = jnp.concatenate([low_core[:, at], high_core[:, at]], axis=1)
        high = value.astype(BF).astype(F32)
        low = value - high
        out_ref[to] = jnp.concatenate([high, low], axis=1).astype(BF)


def root_right_kernel(own_ref, other_ref, s3_ref, s2_ref, s1_ref, out_ref):
    right = (own_ref[...] + other_ref[...]).astype(BF)
    for f in range(FRONTS):
        out_ref[f, :, :1024] = right
    out_ref[:, :, 1024:1152] = s3_ref[...]
    out_ref[:, :, 1152:1280] = s2_ref[...]
    out_ref[:, :, 1280:] = s1_ref[...]


def root_kernel(got_ref, inv_ref, out_ref):
    right = got_ref[:, :, :1024].reshape(256, 1024)
    out_ref[3] = nt(inv_ref[0], right)
    for a in range(3):
        at = 1024 + a * 128
        both = got_ref[:, :, at : at + 128].reshape(256, 128).astype(F32).T
        out_ref[a] = both[:64] + both[64:]


def swap(block, pairs):
    return lax.ppermute(block, "leaf", pairs)


def core_pairs():
    return [(i, i ^ 1) for i in range(16)]


def chip_pairs(level):
    pairs = []
    for i in range(16):
        z, core = i // 2, i % 2
        if level == 0:
            to = z ^ 1
        elif level == 1:
            to = z ^ 2
        else:
            to = (6, 7, 4, 5, 2, 3, 0, 1)[z]
        pairs.append((i, 2 * to + core))
    return pairs


def local(rhs_leaf, rhs_top, inv_leaf, inv_top, off_leaf, off_top, idx_leaf, idx_top):
    leaf = lax.axis_index("leaf")
    front = lax.axis_index("front")
    nodes = [jnp.right_shift(16 + leaf, a + 1) for a in range(4)]
    subs = [leaf & (2 ** (a + 1) - 1) for a in range(4)]
    place = nodes + subs + [leaf & 1, front & 1, front // 4, front % 4]
    place = jnp.stack(place).astype(jnp.int32)
    off_top = jnp.swapaxes(off_top, 1, 2)
    off_leaf = jnp.swapaxes(off_leaf, 1, 2)

    sent, third, pair = first_payload(place, rhs_leaf, rhs_top, inv_top, off_top)
    first = lax.all_to_all(sent, "front", 0, 0)
    pair_near = near(pair, "y")
    pair_far = far(pair_near, "y")
    leaf_x, sent = call(
        leaf_solve_kernel,
        (jax.ShapeDtypeStruct((64, 256), F32), jax.ShapeDtypeStruct((FRONTS, 80, 1024), BF)),
        [VMEM] * 4,
        (inv_leaf, first, off_leaf, third),
    )
    second, lowest = stack((pair, *pair_near, *pair_far))
    sent, second, lowest = lax.optimization_barrier((sent, second, lowest))
    got = lax.all_to_all(sent, "front", 0, 0)
    got, second = lax.optimization_barrier((got, second))
    second_near = near(second, "x")
    state = call(
        leaf_update_kernel,
        jax.ShapeDtypeStruct((64, 1024), F32),
        [SMEM] + [VMEM] * 3,
        (place, first, got, idx_leaf),
    )
    other = swap(state, core_pairs())
    ships = []
    for level in range(3):
        if level == 0:
            parts = (got,)
        elif level == 1:
            parts = (second, *second_near, *second_far)
        else:
            parts = (lowest, *lowest_near, *lowest_far)
        ux, rest = top_solve(state, other, [part.reshape(-1, 80 if level == 0 else 64, 1024) for part in parts])
        ux_other = swap(ux, core_pairs())
        state = call(
            functools.partial(update_kernel, level),
            jax.ShapeDtypeStruct(rest.shape, F32),
            [SMEM] + [VMEM] * 4,
            (place, ux, ux_other, rest, idx_top),
        )
        if level == 0:
            state, second_near = lax.optimization_barrier((state, second_near))
            second_far = far(second_near, "x")
        other = swap(state, chip_pairs(level))
        if level == 0:
            other, lowest = lax.optimization_barrier((other, lowest))
            lowest_near = near(lowest, "x")
            lowest_far = far(lowest_near, "x")
        ships.append(
            call(
                functools.partial(ship_kernel, level > 0),
                jax.ShapeDtypeStruct((16, 16, 128), BF),
                [SMEM, VMEM, VMEM],
                (place, ux, ux_other),
            )
        )
    sent = call(
        root_right_kernel,
        jax.ShapeDtypeStruct((16, 16, 1408), BF),
        [VMEM] * 5,
        (state, other, *ships),
    )
    got = lax.all_to_all(sent, "front", 0, 0)
    ancestors = call(
        root_kernel,
        jax.ShapeDtypeStruct((4, 64, 256), F32),
        [VMEM] * 2,
        (got, inv_top[:1]),
    )
    return (leaf_x[None], ancestors[None])


def solution(mesh):
    placed = (
        P("leaf", "front", None),
        P(None, "front", None),
        P("leaf", "front", None),
        P(None, "front", None),
        P("leaf", None, "front"),
        P(None, None, "front"),
        P("leaf", None),
        P(),
    )
    return jax.shard_map(
        local,
        mesh=mesh,
        in_specs=placed,
        out_specs=(P("leaf", "front", None), P("leaf", None, "front", None)),
        check_vma=False,
    )
```

```python
import functools

import jax
import jax.numpy as jnp
from jax import lax
from jax.experimental import pallas as pl
from jax.experimental.pallas import tpu as pltpu
from jax.sharding import PartitionSpec as P

BF = jnp.bfloat16
F32 = jnp.float32
FRONTS = 16
COLS = 16
WIDTHS = (8, 4, 2, 1)
STARTS = (0, 8, 12, 14)

VMEM = pl.BlockSpec(memory_space=pltpu.VMEM)
SMEM = pl.BlockSpec(memory_space=pltpu.SMEM)
HBM = pl.BlockSpec(memory_space=pltpu.HBM)


def nt(a, b):
    return lax.dot_general(a, b, (((1,), (1,)), ((), ())), preferred_element_type=F32)


def nn(a, b):
    return jnp.dot(a, b, preferred_element_type=F32)


def halves(value):
    high = value.astype(BF)
    low = (value - high.astype(F32)).astype(BF)
    return high, low


def iota(shape, dim):
    return lax.broadcasted_iota(jnp.int32, shape, dim)


def params(mib=12):
    return pltpu.CompilerParams(vmem_limit_bytes=mib * 2**20)


def call(kernel, outs, specs, args, flops=10**8, bytes_accessed=10**6):
    many = isinstance(outs, (tuple, list))
    return pl.pallas_call(
        kernel,
        out_shape=outs,
        in_specs=specs,
        out_specs=tuple(VMEM for _ in outs) if many else VMEM,
        compiler_params=params(),
        cost_estimate=pl.CostEstimate(
            flops=flops, bytes_accessed=bytes_accessed, transcendentals=0
        ),
    )(*args)


def first_kernel(place, leaf_ref, rhs_ref, inv_ref, off_ref, out_ref, *refs):
    third_ref, pair_ref, held, sems = refs
    copies = [
        pltpu.make_async_copy(rhs_ref.at[place[a] - 1], held.at[a], sems.at[a]) for a in range(4)
    ]
    at = pl.ds(pl.multiple_of(place[8] * 32, 32), 32)
    for level, (piece, start) in enumerate(((third_ref, 0), (pair_ref, 0), (pair_ref, 64))):
        node = place[level]
        for part, (ref, index) in enumerate(((inv_ref, node - 1), (off_ref, node - 2))):
            copies.append(
                pltpu.make_async_copy(
                    ref.at[index, at, :],
                    piece.at[pl.ds(start + part * 32, 32), :],
                    sems.at[len(copies)],
                )
            )
    for copy in copies:
        copy.start()
    right = leaf_ref[0].astype(BF)
    for f in range(FRONTS):
        out_ref[f, :64, :] = right
    for copy in copies:
        copy.wait()
    total = jnp.zeros((256, 256), F32)
    to = iota((256, 256), 0)
    come = iota((256, 256), 1)
    slot = to % 16
    odd = place[9].astype(F32)
    even = 1.0 - odd
    for a in range(4):
        sub = place[4 + a]
        width, start = WIDTHS[a], STARTS[a]
        from_col = (to - slot) + sub * width + (slot - start)
        chosen = (slot >= start) & (slot < start + width) & (come == from_col)
        high, low = halves(held[a])
        high = high.astype(F32)
        low = low.astype(F32)
        stacked = jnp.concatenate([high * even, high * odd, low * even, low * odd], axis=0)
        total = total + nt(jnp.where(chosen, 1.0, 0.0).astype(BF), stacked.astype(BF))
    out_ref[:, 64:, :] = total.astype(BF).reshape(16, 16, 256)


def first_payload(place, rhs_leaf, rhs_top, inv_top, off_top):
    return pl.pallas_call(
        first_kernel,
        out_shape=(
            jax.ShapeDtypeStruct((FRONTS, 80, 256), BF),
            jax.ShapeDtypeStruct((64, 1024), BF),
            jax.ShapeDtypeStruct((128, 1024), BF),
        ),
        in_specs=[SMEM, VMEM, HBM, HBM, HBM],
        out_specs=(VMEM,) * 3,
        scratch_shapes=[pltpu.VMEM((4, 64, 256), F32), pltpu.SemaphoreType.DMA((10,))],
        compiler_params=params(60),
    )(place, rhs_leaf, rhs_top, inv_top, off_top)


def stack_kernel(starts, *refs):
    for k, (start, ref) in enumerate(zip(starts, refs)):
        refs[-1][k * 64 : (k + 1) * 64, :] = ref[start : start + 64, :]


def stack(parts, starts):
    return call(
        functools.partial(stack_kernel, starts),
        jax.ShapeDtypeStruct((256, 1024), BF),
        [VMEM] * 4,
        tuple(parts),
    )


def turn(block, dx, dy):
    route = [(i, (i // 4 + dx) % 4 * 4 + (i % 4 + dy) % 4) for i in range(FRONTS)]
    return lax.ppermute(block, "front", route)


def step_of(axis):
    return (1, 0) if axis == "x" else (0, 1)


def near(block, axis):
    dx, dy = step_of(axis)
    return turn(block, dx, dy), turn(block, -dx, -dy)


def opposite(block, axis):
    dx, dy = step_of(axis)
    return turn(block, 2 * dx, 2 * dy)


def far(pair, axis):
    dx, dy = step_of(axis)
    before, after = pair
    half = before.shape[0] // 2
    return turn(after[:half], -dx, -dy), turn(before[half:], dx, dy)


def leaf_solve_kernel(inv_ref, rhs_ref, off_ref, x_ref, out_ref):
    right = rhs_ref[:, :64, :].reshape(1024, 256)
    x = nn(inv_ref[0], right)
    x_ref[...] = x
    xt = x.T.astype(BF)
    update = nn(xt, off_ref[0])
    out_ref[...] = update.astype(BF).reshape(16, 16, 1024)


def push(update, idx, count):
    high, low = halves(update)
    both = jnp.concatenate([high, low], axis=0)
    blocks = []
    step = 512
    for a in range(count):
        parts = []
        for t in range(1024 // step):
            hit = iota((step, 1024), 0) + (a * 1024 + t * step) == idx
            got = nt(both, jnp.where(hit, 1.0, 0.0).astype(BF))
            parts.append(got[:16] + got[16:])
        blocks.append(jnp.concatenate(parts, axis=1))
    return blocks


def leaf_update_kernel(place, first_ref, got_ref, idx_ref, next_ref, rest_ref):
    update = jnp.zeros((16, 1024), F32)
    for s in range(FRONTS):
        update = update + got_ref[s].astype(F32)
    pending = push(update, idx_ref[...], 4)
    high, low = [], []
    for g in range(FRONTS // 2):
        pair = first_ref[2 * g, 64:, :].astype(F32) + first_ref[2 * g + 1, 64:, :].astype(F32)
        high.append(pair[:, :128])
        low.append(pair[:, 128:])
    high = jnp.concatenate(high, axis=1).astype(BF)
    low = jnp.concatenate(low, axis=1).astype(BF)
    row = iota((16, 16), 0)
    slot = iota((16, 16), 1)
    for a in range(4):
        width, start = WIDTHS[a], STARTS[a]
        put = (slot >= start) & (slot < start + width)
        put = put & (row == place[4 + a] * width + slot - start)
        put = jnp.where(put, 1.0, 0.0).astype(BF)
        block = nn(put, high) + nn(put, low) - pending[a]
        if a == 0:
            next_ref[...] = block
        else:
            rest_ref[(a - 1) * 16 : a * 16, :] = block


def solve_kernel(own_ref, other_ref, *refs):
    weights, ux_ref = refs[:-1], refs[-1]
    right = (own_ref[...] + other_ref[...]).astype(BF)
    update = jnp.zeros((16, 1024), F32)
    at = 1024
    for ref in weights:
        rows = ref.shape[0] * 32
        x = nt(right, ref[:, :32, :].reshape(rows, 1024))
        update = update + nn(x.astype(BF), ref[:, 32:, :].reshape(rows, 1024))
        ux_ref[:, at : at + rows] = x
        at += rows
    ux_ref[:, :1024] = update


def top_solve(own, other, weights):
    weights = [part.reshape(-1, 64, 1024) for part in weights]
    return call(
        solve_kernel,
        jax.ShapeDtypeStruct((16, 1536), F32),
        [VMEM] * (2 + len(weights)),
        (own, other, *weights),
    )


def update_kernel(level, place, own_ref, other_ref, left_ref, left_other_ref, idx_ref, *outs):
    update = own_ref[:, :1024] + other_ref[:, :1024]
    count = left_ref.shape[0] // 16
    idx = idx_ref[pl.ds(place[level] - 2, 1), :]
    for a, block in enumerate(push(update, idx, count)):
        at = slice(a * 16, (a + 1) * 16)
        block = left_ref[at, :] + left_other_ref[at, :] - block
        if a == 0:
            outs[0][...] = block
        else:
            outs[1][(a - 1) * 16 : a * 16, :] = block


def top_update(level, place, ux, ux_other, left, left_other, idx_top):
    shapes = [jax.ShapeDtypeStruct((16, 1024), F32)]
    if left.shape[0] > 16:
        shapes.append(jax.ShapeDtypeStruct((left.shape[0] - 16, 1024), F32))
    return call(
        functools.partial(update_kernel, level),
        tuple(shapes),
        [SMEM] + [VMEM] * 5,
        (place, ux, ux_other, left, left_other, idx_top),
    )


def ship_kernel(order, place, own_ref, other_ref, out_ref):
    first = place[8] == 0
    own = own_ref[:, 1024:]
    other = other_ref[:, 1024:]
    low_core = jnp.where(first, own, other)
    high_core = jnp.where(first, other, own)
    for k in range(FRONTS):
        outer, inner = (0, 3, 1, 2)[k // 4], (0, 3, 1, 2)[k % 4]
        if order == "yx":
            to = (place[10] + outer) % 4 * 4 + (place[11] + inner) % 4
        else:
            to = (place[10] + inner) % 4 * 4 + (place[11] + outer) % 4
        at = slice(k * 32, (k + 1) * 32)
        value = jnp.concatenate([low_core[:, at], high_core[:, at]], axis=1)
        high = value.astype(BF).astype(F32)
        low = value - high
        out_ref[to] = jnp.concatenate([high, low], axis=1).astype(BF)


def root_right_kernel(own_ref, other_ref, s3_ref, s2_ref, s1_ref, out_ref):
    right = (own_ref[...] + other_ref[...]).astype(BF)
    for f in range(FRONTS):
        out_ref[f, :, :1024] = right
    out_ref[:, :, 1024:1152] = s3_ref[...]
    out_ref[:, :, 1152:1280] = s2_ref[...]
    out_ref[:, :, 1280:] = s1_ref[...]


def root_kernel(got_ref, inv_ref, out_ref):
    right = got_ref[:, :, :1024].reshape(256, 1024)
    out_ref[3] = nt(inv_ref[0], right)
    for a in range(3):
        at = 1024 + a * 128
        both = got_ref[:, :, at : at + 128].reshape(256, 128).astype(F32).T
        out_ref[a] = both[:64] + both[64:]


def swap(block, pairs):
    return lax.ppermute(block, "leaf", pairs)


def core_pairs():
    return [(i, i ^ 1) for i in range(16)]


def chip_pairs(level):
    pairs = []
    for i in range(16):
        z, core = i // 2, i % 2
        if level == 0:
            to = z ^ 1
        elif level == 1:
            to = z ^ 2
        else:
            to = (6, 7, 4, 5, 2, 3, 0, 1)[z]
        pairs.append((i, 2 * to + core))
    return pairs


def local(rhs_leaf, rhs_top, inv_leaf, inv_top, off_leaf, off_top, idx_leaf, idx_top):
    leaf = lax.axis_index("leaf")
    front = lax.axis_index("front")
    nodes = [jnp.right_shift(16 + leaf, a + 1) for a in range(4)]
    subs = [leaf & (2 ** (a + 1) - 1) for a in range(4)]
    place = nodes + subs + [leaf & 1, front & 1, front // 4, front % 4]
    place = jnp.stack(place).astype(jnp.int32)
    off_top = jnp.swapaxes(off_top, 1, 2)
    off_leaf = jnp.swapaxes(off_leaf, 1, 2)

    sent, third, pair = first_payload(place, rhs_leaf, rhs_top, inv_top, off_top)
    first = lax.all_to_all(sent, "front", 0, 0)
    third = (third, *near(third, "y"), opposite(third, "y"))
    pair = (pair, *near(pair, "x"))
    second = opposite(pair[0][:64], "x")
    leaf_x, sent = call(
        leaf_solve_kernel,
        (jax.ShapeDtypeStruct((64, 256), F32), jax.ShapeDtypeStruct((FRONTS, 16, 1024), BF)),
        [VMEM] * 3,
        (inv_leaf, first, off_leaf),
    )
    sent, third, pair, second = lax.optimization_barrier((sent, third, pair, second))
    got = lax.all_to_all(sent, "front", 0, 0)
    third = stack(third, (0, 0, 0, 0))
    second = stack((*pair, second), (0, 0, 0, 0))
    third_near, second_near = near(third, "x"), near(second, "y")
    lowest = turn(pair[2][64:], -1, 0)
    third_far, second_far = far(third_near, "x"), far(second_near, "y")
    lowest = stack((*pair, lowest), (64, 64, 64, 0))
    got, third_far, second_far, lowest = lax.optimization_barrier(
        (got, third_far, second_far, lowest)
    )
    lowest_near = near(lowest, "y")
    state, left = call(
        leaf_update_kernel,
        (jax.ShapeDtypeStruct((16, 1024), F32), jax.ShapeDtypeStruct((48, 1024), F32)),
        [SMEM] + [VMEM] * 3,
        (place, first, got, idx_leaf),
    )
    other, left_other = swap(state, core_pairs()), swap(left, core_pairs())
    ships = []
    for level in range(3):
        if level == 0:
            parts = (third, *third_near, *third_far)
        elif level == 1:
            parts = (second, *second_near, *second_far)
        else:
            parts = (lowest, *lowest_near, *lowest_far)
        ux = top_solve(state, other, parts)
        if level == 2:
            ux, left_other = lax.optimization_barrier((ux, left_other))
        ux_other = swap(ux, core_pairs())
        state, *more = top_update(level, place, ux, ux_other, left, left_other, idx_top)
        other = swap(state, chip_pairs(level))
        if level == 0:
            other, lowest_near = lax.optimization_barrier((other, lowest_near))
            lowest_far = far(lowest_near, "y")
        if more:
            left, left_other = more[0], swap(more[0], chip_pairs(level))
        ships.append(
            call(
                functools.partial(ship_kernel, ("yx", "xy", "xy")[level]),
                jax.ShapeDtypeStruct((16, 16, 128), BF),
                [SMEM, VMEM, VMEM],
                (place, ux, ux_other),
            )
        )
    sent = call(
        root_right_kernel,
        jax.ShapeDtypeStruct((16, 16, 1408), BF),
        [VMEM] * 5,
        (state, other, *ships),
    )
    got = lax.all_to_all(sent, "front", 0, 0)
    ancestors = call(
        root_kernel,
        jax.ShapeDtypeStruct((4, 64, 256), F32),
        [VMEM] * 2,
        (got, inv_top[:1]),
    )
    return (leaf_x[None], ancestors[None])


def solution(mesh):
    placed = (
        P("leaf", "front", None),
        P(None, "front", None),
        P("leaf", "front", None),
        P(None, "front", None),
        P("leaf", None, "front"),
        P(None, None, "front"),
        P("leaf", None),
        P(),
    )
    return jax.shard_map(
        local,
        mesh=mesh,
        in_specs=placed,
        out_specs=(P("leaf", "front", None), P("leaf", None, "front", None)),
        check_vma=False,
    )
```

```python
import functools

import jax
import jax.numpy as jnp
from jax import lax
from jax.experimental import pallas as pl
from jax.experimental.pallas import tpu as pltpu
from jax.sharding import PartitionSpec as P

BF = jnp.bfloat16
F32 = jnp.float32
FRONTS = 16
COLS = 16
WIDTHS = (8, 4, 2, 1)
STARTS = (0, 8, 12, 14)

VMEM = pl.BlockSpec(memory_space=pltpu.VMEM)
SMEM = pl.BlockSpec(memory_space=pltpu.SMEM)
HBM = pl.BlockSpec(memory_space=pltpu.HBM)


def nt(a, b):
    return lax.dot_general(a, b, (((1,), (1,)), ((), ())), preferred_element_type=F32)


def nn(a, b):
    return jnp.dot(a, b, preferred_element_type=F32)


def halves(value):
    high = value.astype(BF)
    low = (value - high.astype(F32)).astype(BF)
    return high, low


def iota(shape, dim):
    return lax.broadcasted_iota(jnp.int32, shape, dim)


def params(mib=12):
    return pltpu.CompilerParams(vmem_limit_bytes=mib * 2**20)


def call(kernel, outs, specs, args, flops=10**8, bytes_accessed=10**6):
    many = isinstance(outs, (tuple, list))
    return pl.pallas_call(
        kernel,
        out_shape=outs,
        in_specs=specs,
        out_specs=tuple(VMEM for _ in outs) if many else VMEM,
        compiler_params=params(),
        cost_estimate=pl.CostEstimate(
            flops=flops, bytes_accessed=bytes_accessed, transcendentals=0
        ),
    )(*args)


def first_kernel(place, leaf_ref, rhs_ref, inv_ref, off_ref, out_ref, *refs):
    third_ref, pair_ref, held, sems = refs
    copies = [
        pltpu.make_async_copy(rhs_ref.at[place[a] - 1], held.at[a], sems.at[a]) for a in range(4)
    ]
    at = pl.ds(pl.multiple_of(place[8] * 32, 32), 32)
    for level, (piece, start) in enumerate(((third_ref, 0), (pair_ref, 0), (pair_ref, 64))):
        node = place[level]
        for part, (ref, index) in enumerate(((inv_ref, node - 1), (off_ref, node - 2))):
            copies.append(
                pltpu.make_async_copy(
                    ref.at[index, at, :],
                    piece.at[pl.ds(start + part * 32, 32), :],
                    sems.at[len(copies)],
                )
            )
    for copy in copies:
        copy.start()
    right = leaf_ref[0].astype(BF)
    for f in range(FRONTS):
        out_ref[f, :64, :] = right
    for copy in copies:
        copy.wait()
    total = jnp.zeros((256, 256), F32)
    to = iota((256, 256), 0)
    come = iota((256, 256), 1)
    slot = to % 16
    odd = place[9].astype(F32)
    even = 1.0 - odd
    for a in range(4):
        sub = place[4 + a]
        width, start = WIDTHS[a], STARTS[a]
        from_col = (to - slot) + sub * width + (slot - start)
        chosen = (slot >= start) & (slot < start + width) & (come == from_col)
        high, low = halves(held[a])
        high = high.astype(F32)
        low = low.astype(F32)
        stacked = jnp.concatenate([high * even, high * odd, low * even, low * odd], axis=0)
        total = total + nt(jnp.where(chosen, 1.0, 0.0).astype(BF), stacked.astype(BF))
    out_ref[:, 64:, :] = total.astype(BF).reshape(16, 16, 256)


def first_payload(place, rhs_leaf, rhs_top, inv_top, off_top):
    return pl.pallas_call(
        first_kernel,
        out_shape=(
            jax.ShapeDtypeStruct((FRONTS, 80, 256), BF),
            jax.ShapeDtypeStruct((64, 1024), BF),
            jax.ShapeDtypeStruct((128, 1024), BF),
        ),
        in_specs=[SMEM, VMEM, HBM, HBM, HBM],
        out_specs=(VMEM,) * 3,
        scratch_shapes=[pltpu.VMEM((4, 64, 256), F32), pltpu.SemaphoreType.DMA((10,))],
        compiler_params=params(60),
    )(place, rhs_leaf, rhs_top, inv_top, off_top)


def stack_kernel(*refs):
    for k, ref in enumerate(refs[:-1]):
        refs[-1][k * 64 : (k + 1) * 64, :] = ref[...]


def stack(parts):
    return call(
        stack_kernel, jax.ShapeDtypeStruct((256, 1024), BF), [VMEM] * 4, tuple(parts)
    )


def turn(block, dx, dy):
    route = [(i, (i // 4 + dx) % 4 * 4 + (i % 4 + dy) % 4) for i in range(FRONTS)]
    return lax.ppermute(block, "front", route)


def step_of(axis):
    return (1, 0) if axis == "x" else (0, 1)


def near(block, axis):
    dx, dy = step_of(axis)
    return turn(block, dx, dy), turn(block, -dx, -dy)


def opposite(block, axis):
    dx, dy = step_of(axis)
    return turn(block, 2 * dx, 2 * dy)


def far(pair, axis):
    dx, dy = step_of(axis)
    before, after = pair
    half = before.shape[0] // 2
    return turn(after[:half], -dx, -dy), turn(before[half:], dx, dy)


def leaf_solve_kernel(inv_ref, rhs_ref, off_ref, x_ref, out_ref):
    right = rhs_ref[:, :64, :].reshape(1024, 256)
    x = nn(inv_ref[0], right)
    x_ref[...] = x
    xt = x.T.astype(BF)
    update = nn(xt, off_ref[0])
    out_ref[...] = update.astype(BF).reshape(16, 16, 1024)


def push(update, idx, count):
    high, low = halves(update)
    both = jnp.concatenate([high, low], axis=0)
    blocks = []
    step = 512
    for a in range(count):
        parts = []
        for t in range(1024 // step):
            hit = iota((step, 1024), 0) + (a * 1024 + t * step) == idx
            got = nt(both, jnp.where(hit, 1.0, 0.0).astype(BF))
            parts.append(got[:16] + got[16:])
        blocks.append(jnp.concatenate(parts, axis=1))
    return blocks


def leaf_update_kernel(place, first_ref, got_ref, idx_ref, next_ref, rest_ref):
    update = jnp.zeros((16, 1024), F32)
    for s in range(FRONTS):
        update = update + got_ref[s].astype(F32)
    pending = push(update, idx_ref[...], 4)
    high, low = [], []
    for g in range(FRONTS // 2):
        pair = first_ref[2 * g, 64:, :].astype(F32) + first_ref[2 * g + 1, 64:, :].astype(F32)
        high.append(pair[:, :128])
        low.append(pair[:, 128:])
    high = jnp.concatenate(high, axis=1).astype(BF)
    low = jnp.concatenate(low, axis=1).astype(BF)
    row = iota((16, 16), 0)
    slot = iota((16, 16), 1)
    for a in range(4):
        width, start = WIDTHS[a], STARTS[a]
        put = (slot >= start) & (slot < start + width)
        put = put & (row == place[4 + a] * width + slot - start)
        put = jnp.where(put, 1.0, 0.0).astype(BF)
        block = nn(put, high) + nn(put, low) - pending[a]
        if a == 0:
            next_ref[...] = block
        else:
            rest_ref[(a - 1) * 16 : a * 16, :] = block


def solve_kernel(own_ref, other_ref, *refs):
    weights, ux_ref = refs[:-1], refs[-1]
    right = (own_ref[...] + other_ref[...]).astype(BF)
    update = jnp.zeros((16, 1024), F32)
    at = 1024
    for ref in weights:
        rows = ref.shape[0] * 32
        x = nt(right, ref[:, :32, :].reshape(rows, 1024))
        update = update + nn(x.astype(BF), ref[:, 32:, :].reshape(rows, 1024))
        ux_ref[:, at : at + rows] = x
        at += rows
    ux_ref[:, :1024] = update


def top_solve(own, other, weights):
    weights = [part.reshape(-1, 64, 1024) for part in weights]
    return call(
        solve_kernel,
        jax.ShapeDtypeStruct((16, 1536), F32),
        [VMEM] * (2 + len(weights)),
        (own, other, *weights),
    )


def gathered_solve(own, other, weights, level):
    whole = pl.BlockSpec(own.shape, lambda i: (0, 0))
    return pl.pallas_call(
        solve_kernel,
        grid=(1,),
        in_specs=[whole, whole, pl.BlockSpec((FRONTS, 64, 1024), lambda i: (0, level, 0))],
        out_specs=pl.BlockSpec((16, 1536), lambda i: (0, 0)),
        out_shape=jax.ShapeDtypeStruct((16, 1536), F32),
        compiler_params=params(),
    )(own, other, weights)


def update_kernel(level, place, own_ref, other_ref, left_ref, left_other_ref, idx_ref, *outs):
    update = own_ref[:, :1024] + other_ref[:, :1024]
    count = left_ref.shape[0] // 16
    idx = idx_ref[pl.ds(place[level] - 2, 1), :]
    for a, block in enumerate(push(update, idx, count)):
        at = slice(a * 16, (a + 1) * 16)
        block = left_ref[at, :] + left_other_ref[at, :] - block
        if a == 0:
            outs[0][...] = block
        else:
            outs[1][(a - 1) * 16 : a * 16, :] = block


def top_update(level, place, ux, ux_other, left, left_other, idx_top):
    shapes = [jax.ShapeDtypeStruct((16, 1024), F32)]
    if left.shape[0] > 16:
        shapes.append(jax.ShapeDtypeStruct((left.shape[0] - 16, 1024), F32))
    return call(
        functools.partial(update_kernel, level),
        tuple(shapes),
        [SMEM] + [VMEM] * 5,
        (place, ux, ux_other, left, left_other, idx_top),
    )


def ship_kernel(turned, place, own_ref, other_ref, out_ref):
    first = place[8] == 0
    own = own_ref[:, 1024:]
    other = other_ref[:, 1024:]
    low_core = jnp.where(first, own, other)
    high_core = jnp.where(first, other, own)
    for k in range(FRONTS):
        outer, inner = (0, 3, 1, 2)[k // 4], (0, 3, 1, 2)[k % 4]
        to = k
        if turned:
            to = (place[10] + outer) % 4 * 4 + (place[11] + inner) % 4
        at = slice(k * 32, (k + 1) * 32)
        value = jnp.concatenate([low_core[:, at], high_core[:, at]], axis=1)
        high = value.astype(BF).astype(F32)
        low = value - high
        out_ref[to] = jnp.concatenate([high, low], axis=1).astype(BF)


def root_right_kernel(own_ref, other_ref, s3_ref, s2_ref, s1_ref, out_ref):
    right = (own_ref[...] + other_ref[...]).astype(BF)
    for f in range(FRONTS):
        out_ref[f, :, :1024] = right
    out_ref[:, :, 1024:1152] = s3_ref[...]
    out_ref[:, :, 1152:1280] = s2_ref[...]
    out_ref[:, :, 1280:] = s1_ref[...]


def root_kernel(got_ref, inv_ref, out_ref):
    right = got_ref[:, :, :1024].reshape(256, 1024)
    out_ref[3] = nt(inv_ref[0], right)
    for a in range(3):
        at = 1024 + a * 128
        both = got_ref[:, :, at : at + 128].reshape(256, 128).astype(F32).T
        out_ref[a] = both[:64] + both[64:]


def swap(block, pairs):
    return lax.ppermute(block, "leaf", pairs)


def core_pairs():
    return [(i, i ^ 1) for i in range(16)]


def chip_pairs(level):
    pairs = []
    for i in range(16):
        z, core = i // 2, i % 2
        if level == 0:
            to = z ^ 1
        elif level == 1:
            to = z ^ 2
        else:
            to = (6, 7, 4, 5, 2, 3, 0, 1)[z]
        pairs.append((i, 2 * to + core))
    return pairs


def local(rhs_leaf, rhs_top, inv_leaf, inv_top, off_leaf, off_top, idx_leaf, idx_top):
    leaf = lax.axis_index("leaf")
    front = lax.axis_index("front")
    nodes = [jnp.right_shift(16 + leaf, a + 1) for a in range(4)]
    subs = [leaf & (2 ** (a + 1) - 1) for a in range(4)]
    place = nodes + subs + [leaf & 1, front & 1, front // 4, front % 4]
    place = jnp.stack(place).astype(jnp.int32)
    off_top = jnp.swapaxes(off_top, 1, 2)
    off_leaf = jnp.swapaxes(off_leaf, 1, 2)

    sent, third, pair = first_payload(place, rhs_leaf, rhs_top, inv_top, off_top)
    first = lax.all_to_all(sent, "front", 0, 0)
    weights = lax.all_gather(pair, "front", axis=0)
    third = (third, *near(third, "y"), opposite(third, "y"))
    leaf_x, sent = call(
        leaf_solve_kernel,
        (jax.ShapeDtypeStruct((64, 256), F32), jax.ShapeDtypeStruct((FRONTS, 16, 1024), BF)),
        [VMEM] * 3,
        (inv_leaf, first, off_leaf),
    )
    sent, third = lax.optimization_barrier((sent, third))
    got = lax.all_to_all(sent, "front", 0, 0)
    third = stack(third)
    third_near = near(third, "x")
    third_far = far(third_near, "x")
    got, third_far = lax.optimization_barrier((got, third_far))
    state, left = call(
        leaf_update_kernel,
        (jax.ShapeDtypeStruct((16, 1024), F32), jax.ShapeDtypeStruct((48, 1024), F32)),
        [SMEM] + [VMEM] * 3,
        (place, first, got, idx_leaf),
    )
    other, left_other = swap(state, core_pairs()), swap(left, core_pairs())
    ships = []
    for level in range(3):
        if level == 0:
            ux = top_solve(state, other, (third, *third_near, *third_far))
        else:
            ux = gathered_solve(state, other, weights, level - 1)
        if level == 2:
            ux, left_other = lax.optimization_barrier((ux, left_other))
        ux_other = swap(ux, core_pairs())
        state, *more = top_update(level, place, ux, ux_other, left, left_other, idx_top)
        other = swap(state, chip_pairs(level))
        if more:
            left, left_other = more[0], swap(more[0], chip_pairs(level))
        ships.append(
            call(
                functools.partial(ship_kernel, level == 0),
                jax.ShapeDtypeStruct((16, 16, 128), BF),
                [SMEM, VMEM, VMEM],
                (place, ux, ux_other),
            )
        )
    sent = call(
        root_right_kernel,
        jax.ShapeDtypeStruct((16, 16, 1408), BF),
        [VMEM] * 5,
        (state, other, *ships),
    )
    got = lax.all_to_all(sent, "front", 0, 0)
    ancestors = call(
        root_kernel,
        jax.ShapeDtypeStruct((4, 64, 256), F32),
        [VMEM] * 2,
        (got, inv_top[:1]),
    )
    return (leaf_x[None], ancestors[None])


def solution(mesh):
    placed = (
        P("leaf", "front", None),
        P(None, "front", None),
        P("leaf", "front", None),
        P(None, "front", None),
        P("leaf", None, "front"),
        P(None, None, "front"),
        P("leaf", None),
        P(),
    )
    return jax.shard_map(
        local,
        mesh=mesh,
        in_specs=placed,
        out_specs=(P("leaf", "front", None), P("leaf", None, "front", None)),
        check_vma=False,
    )
```

```python
import functools

import jax
import jax.numpy as jnp
from jax import lax
from jax.experimental import pallas as pl
from jax.experimental.pallas import tpu as pltpu
from jax.sharding import PartitionSpec as P

BF = jnp.bfloat16
F32 = jnp.float32
FRONTS = 16
COLS = 16
WIDTHS = (8, 4, 2, 1)
STARTS = (0, 8, 12, 14)

VMEM = pl.BlockSpec(memory_space=pltpu.VMEM)
SMEM = pl.BlockSpec(memory_space=pltpu.SMEM)
HBM = pl.BlockSpec(memory_space=pltpu.HBM)


def nt(a, b):
    return lax.dot_general(a, b, (((1,), (1,)), ((), ())), preferred_element_type=F32)


def nn(a, b):
    return jnp.dot(a, b, preferred_element_type=F32)


def halves(value):
    high = value.astype(BF)
    low = (value - high.astype(F32)).astype(BF)
    return high, low


def iota(shape, dim):
    return lax.broadcasted_iota(jnp.int32, shape, dim)


def params(mib=12):
    return pltpu.CompilerParams(vmem_limit_bytes=mib * 2**20)


def call(kernel, outs, specs, args, flops=10**8, bytes_accessed=10**6):
    many = isinstance(outs, (tuple, list))
    return pl.pallas_call(
        kernel,
        out_shape=outs,
        in_specs=specs,
        out_specs=tuple(VMEM for _ in outs) if many else VMEM,
        compiler_params=params(),
        cost_estimate=pl.CostEstimate(
            flops=flops, bytes_accessed=bytes_accessed, transcendentals=0
        ),
    )(*args)


def first_kernel(place, leaf_ref, rhs_ref, inv_ref, off_ref, out_ref, *refs):
    second_ref, pair_ref, held, sems = refs
    copies = [
        pltpu.make_async_copy(rhs_ref.at[place[a] - 1], held.at[a], sems.at[a]) for a in range(4)
    ]
    at = pl.ds(pl.multiple_of(place[8] * 32, 32), 32)
    for level, (piece, start) in enumerate(((pair_ref, 0), (second_ref, 0), (pair_ref, 64))):
        node = place[level]
        for part, (ref, index) in enumerate(((inv_ref, node - 1), (off_ref, node - 2))):
            copies.append(
                pltpu.make_async_copy(
                    ref.at[index, at, :],
                    piece.at[pl.ds(start + part * 32, 32), :],
                    sems.at[len(copies)],
                )
            )
    for copy in copies:
        copy.start()
    right = leaf_ref[0].astype(BF)
    for f in range(FRONTS):
        out_ref[f, :64, :] = right
    for copy in copies:
        copy.wait()
    total = jnp.zeros((256, 256), F32)
    to = iota((256, 256), 0)
    come = iota((256, 256), 1)
    slot = to % 16
    odd = place[9].astype(F32)
    even = 1.0 - odd
    for a in range(4):
        sub = place[4 + a]
        width, start = WIDTHS[a], STARTS[a]
        from_col = (to - slot) + sub * width + (slot - start)
        chosen = (slot >= start) & (slot < start + width) & (come == from_col)
        high, low = halves(held[a])
        high = high.astype(F32)
        low = low.astype(F32)
        stacked = jnp.concatenate([high * even, high * odd, low * even, low * odd], axis=0)
        total = total + nt(jnp.where(chosen, 1.0, 0.0).astype(BF), stacked.astype(BF))
    out_ref[:, 64:, :] = total.astype(BF).reshape(16, 16, 256)


def first_payload(place, rhs_leaf, rhs_top, inv_top, off_top):
    return pl.pallas_call(
        first_kernel,
        out_shape=(
            jax.ShapeDtypeStruct((FRONTS, 80, 256), BF),
            jax.ShapeDtypeStruct((64, 1024), BF),
            jax.ShapeDtypeStruct((128, 1024), BF),
        ),
        in_specs=[SMEM, VMEM, HBM, HBM, HBM],
        out_specs=(VMEM,) * 3,
        scratch_shapes=[pltpu.VMEM((4, 64, 256), F32), pltpu.SemaphoreType.DMA((10,))],
        compiler_params=params(60),
    )(place, rhs_leaf, rhs_top, inv_top, off_top)


def stack_kernel(starts, *refs):
    for k, (start, ref) in enumerate(zip(starts, refs)):
        refs[-1][k * 64 : (k + 1) * 64, :] = ref[start : start + 64, :]


def stack(parts, starts):
    return call(
        functools.partial(stack_kernel, starts),
        jax.ShapeDtypeStruct((256, 1024), BF),
        [VMEM] * 4,
        tuple(parts),
    )


def turn(block, dx, dy):
    route = [(i, (i // 4 + dx) % 4 * 4 + (i % 4 + dy) % 4) for i in range(FRONTS)]
    return lax.ppermute(block, "front", route)


def step_of(axis):
    return (1, 0) if axis == "x" else (0, 1)


def near(block, axis):
    dx, dy = step_of(axis)
    return turn(block, dx, dy), turn(block, -dx, -dy)


def opposite(block, axis):
    dx, dy = step_of(axis)
    return turn(block, 2 * dx, 2 * dy)


def far(pair, axis):
    dx, dy = step_of(axis)
    before, after = pair
    half = before.shape[0] // 2
    return turn(after[:half], -dx, -dy), turn(before[half:], dx, dy)


def leaf_solve_kernel(inv_ref, rhs_ref, off_ref, x_ref, out_ref):
    right = rhs_ref[:, :64, :].reshape(1024, 256)
    x = nn(inv_ref[0], right)
    x_ref[...] = x
    xt = x.T.astype(BF)
    update = nn(xt, off_ref[0])
    out_ref[...] = update.astype(BF).reshape(16, 16, 1024)


def push(update, idx, count):
    high, low = halves(update)
    both = jnp.concatenate([high, low], axis=0)
    blocks = []
    step = 512
    for a in range(count):
        parts = []
        for t in range(1024 // step):
            hit = iota((step, 1024), 0) + (a * 1024 + t * step) == idx
            got = nt(both, jnp.where(hit, 1.0, 0.0).astype(BF))
            parts.append(got[:16] + got[16:])
        blocks.append(jnp.concatenate(parts, axis=1))
    return blocks


def leaf_update_kernel(place, first_ref, got_ref, idx_ref, next_ref, rest_ref):
    update = jnp.zeros((16, 1024), F32)
    for s in range(FRONTS):
        update = update + got_ref[s].astype(F32)
    pending = push(update, idx_ref[...], 4)
    high, low = [], []
    for g in range(FRONTS // 2):
        pair = first_ref[2 * g, 64:, :].astype(F32) + first_ref[2 * g + 1, 64:, :].astype(F32)
        high.append(pair[:, :128])
        low.append(pair[:, 128:])
    high = jnp.concatenate(high, axis=1).astype(BF)
    low = jnp.concatenate(low, axis=1).astype(BF)
    row = iota((16, 16), 0)
    slot = iota((16, 16), 1)
    for a in range(4):
        width, start = WIDTHS[a], STARTS[a]
        put = (slot >= start) & (slot < start + width)
        put = put & (row == place[4 + a] * width + slot - start)
        put = jnp.where(put, 1.0, 0.0).astype(BF)
        block = nn(put, high) + nn(put, low) - pending[a]
        if a == 0:
            next_ref[...] = block
        else:
            rest_ref[(a - 1) * 16 : a * 16, :] = block


def solve_kernel(own_ref, other_ref, *refs):
    weights, ux_ref = refs[:-1], refs[-1]
    right = (own_ref[...] + other_ref[...]).astype(BF)
    update = jnp.zeros((16, 1024), F32)
    at = 1024
    for ref in weights:
        rows = ref.shape[0] * 32
        x = nt(right, ref[:, :32, :].reshape(rows, 1024))
        update = update + nn(x.astype(BF), ref[:, 32:, :].reshape(rows, 1024))
        ux_ref[:, at : at + rows] = x
        at += rows
    ux_ref[:, :1024] = update


def top_solve(own, other, weights):
    weights = [part.reshape(-1, 64, 1024) for part in weights]
    return call(
        solve_kernel,
        jax.ShapeDtypeStruct((16, 1536), F32),
        [VMEM] * (2 + len(weights)),
        (own, other, *weights),
    )


def update_kernel(level, place, own_ref, other_ref, left_ref, left_other_ref, idx_ref, *outs):
    update = own_ref[:, :1024] + other_ref[:, :1024]
    count = left_ref.shape[0] // 16
    idx = idx_ref[pl.ds(place[level] - 2, 1), :]
    for a, block in enumerate(push(update, idx, count)):
        at = slice(a * 16, (a + 1) * 16)
        block = left_ref[at, :] + left_other_ref[at, :] - block
        if a == 0:
            outs[0][...] = block
        else:
            outs[1][(a - 1) * 16 : a * 16, :] = block


def top_update(level, place, ux, ux_other, left, left_other, idx_top):
    shapes = [jax.ShapeDtypeStruct((16, 1024), F32)]
    if left.shape[0] > 16:
        shapes.append(jax.ShapeDtypeStruct((left.shape[0] - 16, 1024), F32))
    return call(
        functools.partial(update_kernel, level),
        tuple(shapes),
        [SMEM] + [VMEM] * 5,
        (place, ux, ux_other, left, left_other, idx_top),
    )


def ship_kernel(order, place, own_ref, other_ref, out_ref):
    first = place[8] == 0
    own = own_ref[:, 1024:]
    other = other_ref[:, 1024:]
    low_core = jnp.where(first, own, other)
    high_core = jnp.where(first, other, own)
    for k in range(FRONTS):
        outer, inner = (0, 3, 1, 2)[k // 4], (0, 3, 1, 2)[k % 4]
        if order == "yx":
            to = (place[10] + outer) % 4 * 4 + (place[11] + inner) % 4
        else:
            to = (place[10] + inner) % 4 * 4 + (place[11] + outer) % 4
        at = slice(k * 32, (k + 1) * 32)
        value = jnp.concatenate([low_core[:, at], high_core[:, at]], axis=1)
        high = value.astype(BF).astype(F32)
        low = value - high
        out_ref[to] = jnp.concatenate([high, low], axis=1).astype(BF)


def root_right_kernel(own_ref, other_ref, s3_ref, s2_ref, s1_ref, out_ref):
    right = (own_ref[...] + other_ref[...]).astype(BF)
    for f in range(FRONTS):
        out_ref[f, :, :1024] = right
    out_ref[:, :, 1024:1152] = s3_ref[...]
    out_ref[:, :, 1152:1280] = s2_ref[...]
    out_ref[:, :, 1280:] = s1_ref[...]


def root_kernel(got_ref, inv_ref, out_ref):
    right = got_ref[:, :, :1024].reshape(256, 1024)
    out_ref[3] = nt(inv_ref[0], right)
    for a in range(3):
        at = 1024 + a * 128
        both = got_ref[:, :, at : at + 128].reshape(256, 128).astype(F32).T
        out_ref[a] = both[:64] + both[64:]


def swap(block, pairs):
    return lax.ppermute(block, "leaf", pairs)


def core_pairs():
    return [(i, i ^ 1) for i in range(16)]


def chip_pairs(level):
    pairs = []
    for i in range(16):
        z, core = i // 2, i % 2
        if level == 0:
            to = z ^ 1
        elif level == 1:
            to = z ^ 2
        else:
            to = (6, 7, 4, 5, 2, 3, 0, 1)[z]
        pairs.append((i, 2 * to + core))
    return pairs


def local(rhs_leaf, rhs_top, inv_leaf, inv_top, off_leaf, off_top, idx_leaf, idx_top):
    leaf = lax.axis_index("leaf")
    front = lax.axis_index("front")
    nodes = [jnp.right_shift(16 + leaf, a + 1) for a in range(4)]
    subs = [leaf & (2 ** (a + 1) - 1) for a in range(4)]
    place = nodes + subs + [leaf & 1, front & 1, front // 4, front % 4]
    place = jnp.stack(place).astype(jnp.int32)
    off_top = jnp.swapaxes(off_top, 1, 2)
    off_leaf = jnp.swapaxes(off_leaf, 1, 2)

    sent, second, pair = first_payload(place, rhs_leaf, rhs_top, inv_top, off_top)
    first = lax.all_to_all(sent, "front", 0, 0)
    pair = (pair, *near(pair, "y"))
    third = opposite(pair[0][:64], "y")
    second = (second, *near(second, "x"), opposite(second, "x"))
    leaf_x, sent = call(
        leaf_solve_kernel,
        (jax.ShapeDtypeStruct((64, 256), F32), jax.ShapeDtypeStruct((FRONTS, 16, 1024), BF)),
        [VMEM] * 3,
        (inv_leaf, first, off_leaf),
    )
    sent, third, pair, second = lax.optimization_barrier((sent, third, pair, second))
    got = lax.all_to_all(sent, "front", 0, 0)
    third = stack((*pair, third), (0, 0, 0, 0))
    second = stack(second, (0, 0, 0, 0))
    third_near, second_near = near(third, "x"), near(second, "y")
    got, third_near, second_near = lax.optimization_barrier((got, third_near, second_near))
    third_far = far(third_near, "x")
    state, left = call(
        leaf_update_kernel,
        (jax.ShapeDtypeStruct((16, 1024), F32), jax.ShapeDtypeStruct((48, 1024), F32)),
        [SMEM] + [VMEM] * 3,
        (place, first, got, idx_leaf),
    )
    state, second_near, pair = lax.optimization_barrier((state, second_near, pair))
    second_far = far(second_near, "y")
    lowest = turn(pair[2][64:], 0, -1)
    other, left_other = swap(state, core_pairs()), swap(left, core_pairs())
    ships = []
    for level in range(3):
        if level == 0:
            parts = (third, *third_near, *third_far)
        elif level == 1:
            parts = (second, *second_near, *second_far)
        else:
            parts = (lowest, *lowest_near, *lowest_far)
        ux = top_solve(state, other, parts)
        if level == 0:
            ux, lowest = lax.optimization_barrier((ux, lowest))
            lowest = stack((*pair, lowest), (64, 64, 64, 0))
            lowest_near = near(lowest, "x")
        if level == 2:
            ux, left_other = lax.optimization_barrier((ux, left_other))
        ux_other = swap(ux, core_pairs())
        state, *more = top_update(level, place, ux, ux_other, left, left_other, idx_top)
        other = swap(state, chip_pairs(level))
        if level == 0:
            other, lowest_near = lax.optimization_barrier((other, lowest_near))
            lowest_far = far(lowest_near, "x")
        if more:
            left, left_other = more[0], swap(more[0], chip_pairs(level))
        ships.append(
            call(
                functools.partial(ship_kernel, ("yx", "xy", "yx")[level]),
                jax.ShapeDtypeStruct((16, 16, 128), BF),
                [SMEM, VMEM, VMEM],
                (place, ux, ux_other),
            )
        )
    sent = call(
        root_right_kernel,
        jax.ShapeDtypeStruct((16, 16, 1408), BF),
        [VMEM] * 5,
        (state, other, *ships),
    )
    got = lax.all_to_all(sent, "front", 0, 0)
    ancestors = call(
        root_kernel,
        jax.ShapeDtypeStruct((4, 64, 256), F32),
        [VMEM] * 2,
        (got, inv_top[:1]),
    )
    return (leaf_x[None], ancestors[None])


def solution(mesh):
    placed = (
        P("leaf", "front", None),
        P(None, "front", None),
        P("leaf", "front", None),
        P(None, "front", None),
        P("leaf", None, "front"),
        P(None, None, "front"),
        P("leaf", None),
        P(),
    )
    return jax.shard_map(
        local,
        mesh=mesh,
        in_specs=placed,
        out_specs=(P("leaf", "front", None), P("leaf", None, "front", None)),
        check_vma=False,
    )
```

```python
import functools

import jax
import jax.numpy as jnp
from jax import lax
from jax.experimental import pallas as pl
from jax.experimental.pallas import tpu as pltpu
from jax.sharding import PartitionSpec as P

BF = jnp.bfloat16
F32 = jnp.float32
FRONTS = 16
COLS = 16
WIDTHS = (8, 4, 2, 1)
STARTS = (0, 8, 12, 14)

VMEM = pl.BlockSpec(memory_space=pltpu.VMEM)
SMEM = pl.BlockSpec(memory_space=pltpu.SMEM)
HBM = pl.BlockSpec(memory_space=pltpu.HBM)


def nt(a, b):
    return lax.dot_general(a, b, (((1,), (1,)), ((), ())), preferred_element_type=F32)


def nn(a, b):
    return jnp.dot(a, b, preferred_element_type=F32)


def halves(value):
    high = value.astype(BF)
    low = (value - high.astype(F32)).astype(BF)
    return high, low


def iota(shape, dim):
    return lax.broadcasted_iota(jnp.int32, shape, dim)


def params(mib=12):
    return pltpu.CompilerParams(vmem_limit_bytes=mib * 2**20)


def call(kernel, outs, specs, args, flops=10**8, bytes_accessed=10**6):
    many = isinstance(outs, (tuple, list))
    return pl.pallas_call(
        kernel,
        out_shape=outs,
        in_specs=specs,
        out_specs=tuple(VMEM for _ in outs) if many else VMEM,
        compiler_params=params(),
        cost_estimate=pl.CostEstimate(
            flops=flops, bytes_accessed=bytes_accessed, transcendentals=0
        ),
    )(*args)


def first_kernel(place, leaf_ref, rhs_ref, inv_ref, off_ref, out_ref, *refs):
    second_ref, pair_ref, held, sems = refs
    copies = [
        pltpu.make_async_copy(rhs_ref.at[place[a] - 1], held.at[a], sems.at[a]) for a in range(4)
    ]
    at = pl.ds(pl.multiple_of(place[8] * 32, 32), 32)
    for level, (piece, start) in enumerate(((pair_ref, 0), (second_ref, 0), (pair_ref, 64))):
        node = place[level]
        for part, (ref, index) in enumerate(((inv_ref, node - 1), (off_ref, node - 2))):
            copies.append(
                pltpu.make_async_copy(
                    ref.at[index, at, :],
                    piece.at[pl.ds(start + part * 32, 32), :],
                    sems.at[len(copies)],
                )
            )
    for copy in copies:
        copy.start()
    right = leaf_ref[0].astype(BF)
    for f in range(FRONTS):
        out_ref[f, :64, :] = right
    for copy in copies:
        copy.wait()
    total = jnp.zeros((256, 256), F32)
    to = iota((256, 256), 0)
    come = iota((256, 256), 1)
    slot = to % 16
    odd = place[9].astype(F32)
    even = 1.0 - odd
    for a in range(4):
        sub = place[4 + a]
        width, start = WIDTHS[a], STARTS[a]
        from_col = (to - slot) + sub * width + (slot - start)
        chosen = (slot >= start) & (slot < start + width) & (come == from_col)
        high, low = halves(held[a])
        high = high.astype(F32)
        low = low.astype(F32)
        stacked = jnp.concatenate([high * even, high * odd, low * even, low * odd], axis=0)
        total = total + nt(jnp.where(chosen, 1.0, 0.0).astype(BF), stacked.astype(BF))
    out_ref[:, 64:, :] = total.astype(BF).reshape(16, 16, 256)


def first_payload(place, rhs_leaf, rhs_top, inv_top, off_top):
    return pl.pallas_call(
        first_kernel,
        out_shape=(
            jax.ShapeDtypeStruct((FRONTS, 80, 256), BF),
            jax.ShapeDtypeStruct((64, 1024), BF),
            jax.ShapeDtypeStruct((128, 1024), BF),
        ),
        in_specs=[SMEM, VMEM, HBM, HBM, HBM],
        out_specs=(VMEM,) * 3,
        scratch_shapes=[pltpu.VMEM((4, 64, 256), F32), pltpu.SemaphoreType.DMA((10,))],
        compiler_params=params(60),
    )(place, rhs_leaf, rhs_top, inv_top, off_top)


def stack_kernel(start, *refs):
    for k, ref in enumerate(refs[:-1]):
        refs[-1][k * 64 : (k + 1) * 64, :] = ref[start : start + 64, :]


def stack(parts, start):
    return call(
        functools.partial(stack_kernel, start),
        jax.ShapeDtypeStruct((256, 1024), BF),
        [VMEM] * 4,
        tuple(parts),
    )


def turn(block, dx, dy):
    route = [(i, (i // 4 + dx) % 4 * 4 + (i % 4 + dy) % 4) for i in range(FRONTS)]
    return lax.ppermute(block, "front", route)


def step_of(axis):
    return (1, 0) if axis == "x" else (0, 1)


def near(block, axis):
    dx, dy = step_of(axis)
    return turn(block, dx, dy), turn(block, -dx, -dy)


def opposite(block, axis):
    dx, dy = step_of(axis)
    return turn(block, 2 * dx, 2 * dy)


def far(pair, axis):
    dx, dy = step_of(axis)
    before, after = pair
    half = before.shape[0] // 2
    return turn(after[:half], -dx, -dy), turn(before[half:], dx, dy)


def leaf_solve_kernel(inv_ref, rhs_ref, off_ref, x_ref, out_ref):
    right = rhs_ref[:, :64, :].reshape(1024, 256)
    x = nn(inv_ref[0], right)
    x_ref[...] = x
    xt = x.T.astype(BF)
    update = nn(xt, off_ref[0])
    out_ref[...] = update.astype(BF).reshape(16, 16, 1024)


def push(update, idx, count):
    high, low = halves(update)
    both = jnp.concatenate([high, low], axis=0)
    blocks = []
    step = 512
    for a in range(count):
        parts = []
        for t in range(1024 // step):
            hit = iota((step, 1024), 0) + (a * 1024 + t * step) == idx
            got = nt(both, jnp.where(hit, 1.0, 0.0).astype(BF))
            parts.append(got[:16] + got[16:])
        blocks.append(jnp.concatenate(parts, axis=1))
    return blocks


def leaf_update_kernel(place, first_ref, got_ref, idx_ref, next_ref, rest_ref):
    update = jnp.zeros((16, 1024), F32)
    for s in range(FRONTS):
        update = update + got_ref[s].astype(F32)
    pending = push(update, idx_ref[...], 4)
    high, low = [], []
    for g in range(FRONTS // 2):
        pair = first_ref[2 * g, 64:, :].astype(F32) + first_ref[2 * g + 1, 64:, :].astype(F32)
        high.append(pair[:, :128])
        low.append(pair[:, 128:])
    high = jnp.concatenate(high, axis=1).astype(BF)
    low = jnp.concatenate(low, axis=1).astype(BF)
    row = iota((16, 16), 0)
    slot = iota((16, 16), 1)
    for a in range(4):
        width, start = WIDTHS[a], STARTS[a]
        put = (slot >= start) & (slot < start + width)
        put = put & (row == place[4 + a] * width + slot - start)
        put = jnp.where(put, 1.0, 0.0).astype(BF)
        block = nn(put, high) + nn(put, low) - pending[a]
        if a == 0:
            next_ref[...] = block
        else:
            rest_ref[(a - 1) * 16 : a * 16, :] = block


def solve_kernel(own_ref, other_ref, *refs):
    weights, ux_ref = refs[:-1], refs[-1]
    right = (own_ref[...] + other_ref[...]).astype(BF)
    update = jnp.zeros((16, 1024), F32)
    at = 1024
    for ref in weights:
        rows = ref.shape[0] * 32
        x = nt(right, ref[:, :32, :].reshape(rows, 1024))
        update = update + nn(x.astype(BF), ref[:, 32:, :].reshape(rows, 1024))
        ux_ref[:, at : at + rows] = x
        at += rows
    ux_ref[:, :1024] = update


def top_solve(own, other, weights):
    weights = [part.reshape(-1, 64, 1024) for part in weights]
    return call(
        solve_kernel,
        jax.ShapeDtypeStruct((16, 1536), F32),
        [VMEM] * (2 + len(weights)),
        (own, other, *weights),
    )


def update_kernel(level, place, own_ref, other_ref, left_ref, left_other_ref, idx_ref, *outs):
    update = own_ref[:, :1024] + other_ref[:, :1024]
    count = left_ref.shape[0] // 16
    idx = idx_ref[pl.ds(place[level] - 2, 1), :]
    for a, block in enumerate(push(update, idx, count)):
        at = slice(a * 16, (a + 1) * 16)
        block = left_ref[at, :] + left_other_ref[at, :] - block
        if a == 0:
            outs[0][...] = block
        else:
            outs[1][(a - 1) * 16 : a * 16, :] = block


def top_update(level, place, ux, ux_other, left, left_other, idx_top):
    shapes = [jax.ShapeDtypeStruct((16, 1024), F32)]
    if left.shape[0] > 16:
        shapes.append(jax.ShapeDtypeStruct((left.shape[0] - 16, 1024), F32))
    return call(
        functools.partial(update_kernel, level),
        tuple(shapes),
        [SMEM] + [VMEM] * 5,
        (place, ux, ux_other, left, left_other, idx_top),
    )


def ship_kernel(order, place, own_ref, other_ref, out_ref):
    first = place[8] == 0
    own = own_ref[:, 1024:]
    other = other_ref[:, 1024:]
    low_core = jnp.where(first, own, other)
    high_core = jnp.where(first, other, own)
    for k in range(FRONTS):
        outer, inner = (0, 3, 1, 2)[k // 4], (0, 3, 1, 2)[k % 4]
        if order == "yx":
            to = (place[10] + outer) % 4 * 4 + (place[11] + inner) % 4
        else:
            to = (place[10] + inner) % 4 * 4 + (place[11] + outer) % 4
        at = slice(k * 32, (k + 1) * 32)
        value = jnp.concatenate([low_core[:, at], high_core[:, at]], axis=1)
        high = value.astype(BF).astype(F32)
        low = value - high
        out_ref[to] = jnp.concatenate([high, low], axis=1).astype(BF)


def root_right_kernel(own_ref, other_ref, s3_ref, s2_ref, s1_ref, out_ref):
    right = (own_ref[...] + other_ref[...]).astype(BF)
    for f in range(FRONTS):
        out_ref[f, :, :1024] = right
    out_ref[:, :, 1024:1152] = s3_ref[...]
    out_ref[:, :, 1152:1280] = s2_ref[...]
    out_ref[:, :, 1280:] = s1_ref[...]


def root_kernel(got_ref, inv_ref, out_ref):
    right = got_ref[:, :, :1024].reshape(256, 1024)
    out_ref[3] = nt(inv_ref[0], right)
    for a in range(3):
        at = 1024 + a * 128
        both = got_ref[:, :, at : at + 128].reshape(256, 128).astype(F32).T
        out_ref[a] = both[:64] + both[64:]


def swap(block, pairs):
    return lax.ppermute(block, "leaf", pairs)


def core_pairs():
    return [(i, i ^ 1) for i in range(16)]


def chip_pairs(level):
    pairs = []
    for i in range(16):
        z, core = i // 2, i % 2
        if level == 0:
            to = z ^ 1
        elif level == 1:
            to = z ^ 2
        else:
            to = (6, 7, 4, 5, 2, 3, 0, 1)[z]
        pairs.append((i, 2 * to + core))
    return pairs


def local(rhs_leaf, rhs_top, inv_leaf, inv_top, off_leaf, off_top, idx_leaf, idx_top):
    leaf = lax.axis_index("leaf")
    front = lax.axis_index("front")
    nodes = [jnp.right_shift(16 + leaf, a + 1) for a in range(4)]
    subs = [leaf & (2 ** (a + 1) - 1) for a in range(4)]
    place = nodes + subs + [leaf & 1, front & 1, front // 4, front % 4]
    place = jnp.stack(place).astype(jnp.int32)
    off_top = jnp.swapaxes(off_top, 1, 2)
    off_leaf = jnp.swapaxes(off_leaf, 1, 2)

    sent, second, pair = first_payload(place, rhs_leaf, rhs_top, inv_top, off_top)
    first = lax.all_to_all(sent, "front", 0, 0)
    pair = (pair, *near(pair, "y"))
    pair = (*pair, opposite(pair[0], "y"))
    second = (second, *near(second, "x"), opposite(second, "x"))
    leaf_x, sent = call(
        leaf_solve_kernel,
        (jax.ShapeDtypeStruct((64, 256), F32), jax.ShapeDtypeStruct((FRONTS, 16, 1024), BF)),
        [VMEM] * 3,
        (inv_leaf, first, off_leaf),
    )
    sent, pair, second = lax.optimization_barrier((sent, pair, second))
    got = lax.all_to_all(sent, "front", 0, 0)
    third, second = stack(pair, 0), stack(second, 0)
    third_near, second_near = near(third, "x"), near(second, "y")
    got, third_near, second_near, pair = lax.optimization_barrier(
        (got, third_near, second_near, pair)
    )
    lowest = stack(pair, 64)
    third_far = far(third_near, "x")
    state, left = call(
        leaf_update_kernel,
        (jax.ShapeDtypeStruct((16, 1024), F32), jax.ShapeDtypeStruct((48, 1024), F32)),
        [SMEM] + [VMEM] * 3,
        (place, first, got, idx_leaf),
    )
    state, second_near = lax.optimization_barrier((state, second_near))
    second_far = far(second_near, "y")
    other, left_other = swap(state, core_pairs()), swap(left, core_pairs())
    ships = []
    for level in range(3):
        if level == 0:
            parts = (third, *third_near, *third_far)
        elif level == 1:
            parts = (second, *second_near, *second_far)
        else:
            parts = (lowest, *lowest_near, *lowest_far)
        ux = top_solve(state, other, parts)
        if level == 0:
            ux, lowest = lax.optimization_barrier((ux, lowest))
            lowest_near = near(lowest, "x")
        if level > 0:
            ux, left_other = lax.optimization_barrier((ux, left_other))
        ux_other = swap(ux, core_pairs())
        state, *more = top_update(level, place, ux, ux_other, left, left_other, idx_top)
        other = swap(state, chip_pairs(level))
        if level == 0:
            other, lowest_near = lax.optimization_barrier((other, lowest_near))
            lowest_far = far(lowest_near, "x")
        if more:
            left, left_other = more[0], swap(more[0], chip_pairs(level))
        ships.append(
            call(
                functools.partial(ship_kernel, ("yx", "xy", "yx")[level]),
                jax.ShapeDtypeStruct((16, 16, 128), BF),
                [SMEM, VMEM, VMEM],
                (place, ux, ux_other),
            )
        )
    sent = call(
        root_right_kernel,
        jax.ShapeDtypeStruct((16, 16, 1408), BF),
        [VMEM] * 5,
        (state, other, *ships),
    )
    got = lax.all_to_all(sent, "front", 0, 0)
    ancestors = call(
        root_kernel,
        jax.ShapeDtypeStruct((4, 64, 256), F32),
        [VMEM] * 2,
        (got, inv_top[:1]),
    )
    return (leaf_x[None], ancestors[None])


def solution(mesh):
    placed = (
        P("leaf", "front", None),
        P(None, "front", None),
        P("leaf", "front", None),
        P(None, "front", None),
        P("leaf", None, "front"),
        P(None, None, "front"),
        P("leaf", None),
        P(),
    )
    return jax.shard_map(
        local,
        mesh=mesh,
        in_specs=placed,
        out_specs=(P("leaf", "front", None), P("leaf", None, "front", None)),
        check_vma=False,
    )
```

```python
import functools

import jax
import jax.numpy as jnp
from jax import lax
from jax.experimental import pallas as pl
from jax.experimental.pallas import tpu as pltpu
from jax.sharding import PartitionSpec as P

BF = jnp.bfloat16
F32 = jnp.float32
FRONTS = 16
COLS = 16
WIDTHS = (8, 4, 2, 1)
STARTS = (0, 8, 12, 14)

VMEM = pl.BlockSpec(memory_space=pltpu.VMEM)
SMEM = pl.BlockSpec(memory_space=pltpu.SMEM)
HBM = pl.BlockSpec(memory_space=pltpu.HBM)


def nt(a, b):
    return lax.dot_general(a, b, (((1,), (1,)), ((), ())), preferred_element_type=F32)


def nn(a, b):
    return jnp.dot(a, b, preferred_element_type=F32)


def halves(value):
    high = value.astype(BF)
    low = (value - high.astype(F32)).astype(BF)
    return high, low


def iota(shape, dim):
    return lax.broadcasted_iota(jnp.int32, shape, dim)


def params(mib=12):
    return pltpu.CompilerParams(vmem_limit_bytes=mib * 2**20)


def call(kernel, outs, specs, args, flops=10**8, bytes_accessed=10**6):
    many = isinstance(outs, (tuple, list))
    return pl.pallas_call(
        kernel,
        out_shape=outs,
        in_specs=specs,
        out_specs=tuple(VMEM for _ in outs) if many else VMEM,
        compiler_params=params(),
        cost_estimate=pl.CostEstimate(
            flops=flops, bytes_accessed=bytes_accessed, transcendentals=0
        ),
    )(*args)


def first_kernel(place, leaf_ref, rhs_ref, inv_ref, off_ref, out_ref, *refs):
    second_ref, pair_ref, held, sems = refs
    copies = [
        pltpu.make_async_copy(rhs_ref.at[place[a] - 1], held.at[a], sems.at[a]) for a in range(4)
    ]
    at = pl.ds(pl.multiple_of(place[8] * 32, 32), 32)
    for level, (piece, start) in enumerate(((pair_ref, 0), (second_ref, 0), (pair_ref, 64))):
        node = place[level]
        for part, (ref, index) in enumerate(((inv_ref, node - 1), (off_ref, node - 2))):
            copies.append(
                pltpu.make_async_copy(
                    ref.at[index, at, :],
                    piece.at[pl.ds(start + part * 32, 32), :],
                    sems.at[len(copies)],
                )
            )
    for copy in copies:
        copy.start()
    right = leaf_ref[0].astype(BF)
    for f in range(FRONTS):
        out_ref[f, :64, :] = right
    for copy in copies:
        copy.wait()
    total = jnp.zeros((256, 256), F32)
    to = iota((256, 256), 0)
    come = iota((256, 256), 1)
    slot = to % 16
    odd = place[9].astype(F32)
    even = 1.0 - odd
    for a in range(4):
        sub = place[4 + a]
        width, start = WIDTHS[a], STARTS[a]
        from_col = (to - slot) + sub * width + (slot - start)
        chosen = (slot >= start) & (slot < start + width) & (come == from_col)
        high, low = halves(held[a])
        high = high.astype(F32)
        low = low.astype(F32)
        stacked = jnp.concatenate([high * even, high * odd, low * even, low * odd], axis=0)
        total = total + nt(jnp.where(chosen, 1.0, 0.0).astype(BF), stacked.astype(BF))
    out_ref[:, 64:, :] = total.astype(BF).reshape(16, 16, 256)


def first_payload(place, rhs_leaf, rhs_top, inv_top, off_top):
    return pl.pallas_call(
        first_kernel,
        out_shape=(
            jax.ShapeDtypeStruct((FRONTS, 80, 256), BF),
            jax.ShapeDtypeStruct((64, 1024), BF),
            jax.ShapeDtypeStruct((128, 1024), BF),
        ),
        in_specs=[SMEM, VMEM, HBM, HBM, HBM],
        out_specs=(VMEM,) * 3,
        scratch_shapes=[pltpu.VMEM((4, 64, 256), F32), pltpu.SemaphoreType.DMA((10,))],
        compiler_params=params(60),
    )(place, rhs_leaf, rhs_top, inv_top, off_top)


def stack_kernel(start, *refs):
    for k, ref in enumerate(refs[:-1]):
        refs[-1][k * 64 : (k + 1) * 64, :] = ref[start : start + 64, :]


def stack(parts, start):
    return call(
        functools.partial(stack_kernel, start),
        jax.ShapeDtypeStruct((256, 1024), BF),
        [VMEM] * 4,
        tuple(parts),
    )


def turn(block, dx, dy):
    route = [(i, (i // 4 + dx) % 4 * 4 + (i % 4 + dy) % 4) for i in range(FRONTS)]
    return lax.ppermute(block, "front", route)


def step_of(axis):
    return (1, 0) if axis == "x" else (0, 1)


def near(block, axis):
    dx, dy = step_of(axis)
    return turn(block, dx, dy), turn(block, -dx, -dy)


def opposite(block, axis):
    dx, dy = step_of(axis)
    return turn(block, 2 * dx, 2 * dy)


def far(pair, axis):
    dx, dy = step_of(axis)
    before, after = pair
    half = before.shape[0] // 2
    return turn(after[:half], -dx, -dy), turn(before[half:], dx, dy)


def leaf_solve_kernel(inv_ref, rhs_ref, off_ref, x_ref, out_ref):
    right = rhs_ref[:, :64, :].reshape(1024, 256)
    x = nn(inv_ref[0], right)
    x_ref[...] = x
    xt = x.T.astype(BF)
    update = nn(xt, off_ref[0])
    out_ref[...] = update.astype(BF).reshape(16, 16, 1024)


def push(update, idx, ancestors):
    high, low = halves(update)
    both = jnp.concatenate([high, low], axis=0)
    blocks = []
    step = 512
    for a in ancestors:
        parts = []
        for t in range(1024 // step):
            hit = iota((step, 1024), 0) + (a * 1024 + t * step) == idx
            got = nt(both, jnp.where(hit, 1.0, 0.0).astype(BF))
            parts.append(got[:16] + got[16:])
        blocks.append(jnp.concatenate(parts, axis=1))
    return blocks


def leaf_update_kernel(ancestors, place, first_ref, got_ref, idx_ref, out_ref):
    update = jnp.zeros((16, 1024), F32)
    for s in range(FRONTS):
        update = update + got_ref[s].astype(F32)
    pending = push(update, idx_ref[...], ancestors)
    high, low = [], []
    for g in range(FRONTS // 2):
        pair = first_ref[2 * g, 64:, :].astype(F32) + first_ref[2 * g + 1, 64:, :].astype(F32)
        high.append(pair[:, :128])
        low.append(pair[:, 128:])
    high = jnp.concatenate(high, axis=1).astype(BF)
    low = jnp.concatenate(low, axis=1).astype(BF)
    row = iota((16, 16), 0)
    slot = iota((16, 16), 1)
    for k, a in enumerate(ancestors):
        width, start = WIDTHS[a], STARTS[a]
        put = (slot >= start) & (slot < start + width)
        put = put & (row == place[4 + a] * width + slot - start)
        put = jnp.where(put, 1.0, 0.0).astype(BF)
        out_ref[k * 16 : (k + 1) * 16, :] = nn(put, high) + nn(put, low) - pending[k]


def leaf_update(place, first, got, idx_leaf, ancestors):
    return call(
        functools.partial(leaf_update_kernel, ancestors),
        jax.ShapeDtypeStruct((16 * len(ancestors), 1024), F32),
        [SMEM] + [VMEM] * 3,
        (place, first, got, idx_leaf),
    )


def solve_kernel(own_ref, other_ref, *refs):
    weights, ux_ref = refs[:-1], refs[-1]
    right = (own_ref[...] + other_ref[...]).astype(BF)
    update = jnp.zeros((16, 1024), F32)
    at = 1024
    for ref in weights:
        rows = ref.shape[0] * 32
        x = nt(right, ref[:, :32, :].reshape(rows, 1024))
        update = update + nn(x.astype(BF), ref[:, 32:, :].reshape(rows, 1024))
        ux_ref[:, at : at + rows] = x
        at += rows
    ux_ref[:, :1024] = update


def top_solve(own, other, weights):
    weights = [part.reshape(-1, 64, 1024) for part in weights]
    return call(
        solve_kernel,
        jax.ShapeDtypeStruct((16, 1536), F32),
        [VMEM] * (2 + len(weights)),
        (own, other, *weights),
    )


def update_kernel(level, ancestors, place, own_ref, other_ref, left_ref, left_other_ref, idx_ref, out_ref):
    update = own_ref[:, :1024] + other_ref[:, :1024]
    idx = idx_ref[pl.ds(place[level] - 2, 1), :]
    for k, (a, block) in enumerate(zip(ancestors, push(update, idx, ancestors))):
        at = slice(a * 16, (a + 1) * 16)
        out_ref[k * 16 : (k + 1) * 16, :] = left_ref[at, :] + left_other_ref[at, :] - block


def top_update(level, ancestors, args):
    return call(
        functools.partial(update_kernel, level, ancestors),
        jax.ShapeDtypeStruct((16 * len(ancestors), 1024), F32),
        [SMEM] + [VMEM] * 5,
        args,
    )


def ship_kernel(order, place, own_ref, other_ref, out_ref):
    first = place[8] == 0
    own = own_ref[:, 1024:]
    other = other_ref[:, 1024:]
    low_core = jnp.where(first, own, other)
    high_core = jnp.where(first, other, own)
    for k in range(FRONTS):
        outer, inner = (0, 3, 1, 2)[k // 4], (0, 3, 1, 2)[k % 4]
        if order == "yx":
            to = (place[10] + outer) % 4 * 4 + (place[11] + inner) % 4
        else:
            to = (place[10] + inner) % 4 * 4 + (place[11] + outer) % 4
        at = slice(k * 32, (k + 1) * 32)
        value = jnp.concatenate([low_core[:, at], high_core[:, at]], axis=1)
        high = value.astype(BF).astype(F32)
        low = value - high
        out_ref[to] = jnp.concatenate([high, low], axis=1).astype(BF)


def root_right_kernel(own_ref, other_ref, s3_ref, s2_ref, s1_ref, out_ref):
    right = (own_ref[...] + other_ref[...]).astype(BF)
    for f in range(FRONTS):
        out_ref[f, :, :1024] = right
    out_ref[:, :, 1024:1152] = s3_ref[...]
    out_ref[:, :, 1152:1280] = s2_ref[...]
    out_ref[:, :, 1280:] = s1_ref[...]


def root_kernel(got_ref, inv_ref, out_ref):
    right = got_ref[:, :, :1024].reshape(256, 1024)
    out_ref[3] = nt(inv_ref[0], right)
    for a in range(3):
        at = 1024 + a * 128
        both = got_ref[:, :, at : at + 128].reshape(256, 128).astype(F32).T
        out_ref[a] = both[:64] + both[64:]


def swap(block, pairs):
    return lax.ppermute(block, "leaf", pairs)


def core_pairs():
    return [(i, i ^ 1) for i in range(16)]


def chip_pairs(level):
    pairs = []
    for i in range(16):
        z, core = i // 2, i % 2
        if level == 0:
            to = z ^ 1
        elif level == 1:
            to = z ^ 2
        else:
            to = (6, 7, 4, 5, 2, 3, 0, 1)[z]
        pairs.append((i, 2 * to + core))
    return pairs


def local(rhs_leaf, rhs_top, inv_leaf, inv_top, off_leaf, off_top, idx_leaf, idx_top):
    leaf = lax.axis_index("leaf")
    front = lax.axis_index("front")
    nodes = [jnp.right_shift(16 + leaf, a + 1) for a in range(4)]
    subs = [leaf & (2 ** (a + 1) - 1) for a in range(4)]
    place = nodes + subs + [leaf & 1, front & 1, front // 4, front % 4]
    place = jnp.stack(place).astype(jnp.int32)
    off_top = jnp.swapaxes(off_top, 1, 2)
    off_leaf = jnp.swapaxes(off_leaf, 1, 2)

    sent, second, pair = first_payload(place, rhs_leaf, rhs_top, inv_top, off_top)
    first = lax.all_to_all(sent, "front", 0, 0)
    pair = (pair, *near(pair, "y"))
    pair = (*pair, opposite(pair[0], "y"))
    second = (second, *near(second, "x"), opposite(second, "x"))
    leaf_x, sent = call(
        leaf_solve_kernel,
        (jax.ShapeDtypeStruct((64, 256), F32), jax.ShapeDtypeStruct((FRONTS, 16, 1024), BF)),
        [VMEM] * 3,
        (inv_leaf, first, off_leaf),
    )
    sent, pair, second = lax.optimization_barrier((sent, pair, second))
    got = lax.all_to_all(sent, "front", 0, 0)
    third, second = stack(pair, 0), stack(second, 0)
    third_near, second_near = near(third, "x"), near(second, "y")
    got, third_near, second_near, pair = lax.optimization_barrier(
        (got, third_near, second_near, pair)
    )
    lowest = stack(pair, 64)
    third_far = far(third_near, "x")
    state = leaf_update(place, first, got, idx_leaf, (0,))
    left = leaf_update(place, first, got, idx_leaf, (1, 2, 3))
    state, second_near = lax.optimization_barrier((state, second_near))
    second_far = far(second_near, "y")
    other, left = lax.optimization_barrier((swap(state, core_pairs()), left))
    left_other = swap(left, core_pairs())
    ships = []
    for level in range(3):
        if level == 0:
            parts = (third, *third_near, *third_far)
        elif level == 1:
            parts = (second, *second_near, *second_far)
        else:
            parts = (lowest, *lowest_near, *lowest_far)
        ux = top_solve(state, other, parts)
        if level == 0:
            ux, lowest = lax.optimization_barrier((ux, lowest))
            lowest_near = near(lowest, "x")
        if level > 0:
            ux, left_other = lax.optimization_barrier((ux, left_other))
        ux_other = swap(ux, core_pairs())
        args = (place, ux, ux_other, left, left_other, idx_top)
        state = top_update(level, (0,), args)
        other = swap(state, chip_pairs(level))
        if level == 0:
            other, lowest_near = lax.optimization_barrier((other, lowest_near))
            lowest_far = far(lowest_near, "x")
        if level < 2:
            left = top_update(level, tuple(range(1, 3 - level)), args)
            left_other = swap(left, chip_pairs(level))
        ships.append(
            call(
                functools.partial(ship_kernel, ("yx", "xy", "yx")[level]),
                jax.ShapeDtypeStruct((16, 16, 128), BF),
                [SMEM, VMEM, VMEM],
                (place, ux, ux_other),
            )
        )
    sent = call(
        root_right_kernel,
        jax.ShapeDtypeStruct((16, 16, 1408), BF),
        [VMEM] * 5,
        (state, other, *ships),
    )
    got = lax.all_to_all(sent, "front", 0, 0)
    ancestors = call(
        root_kernel,
        jax.ShapeDtypeStruct((4, 64, 256), F32),
        [VMEM] * 2,
        (got, inv_top[:1]),
    )
    return (leaf_x[None], ancestors[None])


def solution(mesh):
    placed = (
        P("leaf", "front", None),
        P(None, "front", None),
        P("leaf", "front", None),
        P(None, "front", None),
        P("leaf", None, "front"),
        P(None, None, "front"),
        P("leaf", None),
        P(),
    )
    return jax.shard_map(
        local,
        mesh=mesh,
        in_specs=placed,
        out_specs=(P("leaf", "front", None), P("leaf", None, "front", None)),
        check_vma=False,
    )
```

```python
import functools

import jax
import jax.numpy as jnp
from jax import lax
from jax.experimental import pallas as pl
from jax.experimental.pallas import tpu as pltpu
from jax.sharding import PartitionSpec as P

BF = jnp.bfloat16
F32 = jnp.float32
FRONTS = 16
COLS = 16
WIDTHS = (8, 4, 2, 1)
STARTS = (0, 8, 12, 14)

VMEM = pl.BlockSpec(memory_space=pltpu.VMEM)
SMEM = pl.BlockSpec(memory_space=pltpu.SMEM)
HBM = pl.BlockSpec(memory_space=pltpu.HBM)


def nt(a, b):
    return lax.dot_general(a, b, (((1,), (1,)), ((), ())), preferred_element_type=F32)


def nn(a, b):
    return jnp.dot(a, b, preferred_element_type=F32)


def halves(value):
    high = value.astype(BF)
    low = (value - high.astype(F32)).astype(BF)
    return high, low


def iota(shape, dim):
    return lax.broadcasted_iota(jnp.int32, shape, dim)


def params(mib=12):
    return pltpu.CompilerParams(vmem_limit_bytes=mib * 2**20)


def call(kernel, outs, specs, args, flops=10**8, bytes_accessed=10**6):
    many = isinstance(outs, (tuple, list))
    return pl.pallas_call(
        kernel,
        out_shape=outs,
        in_specs=specs,
        out_specs=tuple(VMEM for _ in outs) if many else VMEM,
        compiler_params=params(),
        cost_estimate=pl.CostEstimate(
            flops=flops, bytes_accessed=bytes_accessed, transcendentals=0
        ),
    )(*args)


def first_kernel(place, leaf_ref, rhs_ref, inv_ref, off_ref, out_ref, *refs):
    second_ref, pair_ref, held, sems = refs
    copies = [
        pltpu.make_async_copy(rhs_ref.at[place[a] - 1], held.at[a], sems.at[a]) for a in range(4)
    ]
    at = pl.ds(pl.multiple_of(place[8] * 32, 32), 32)
    for level, (piece, start) in enumerate(((pair_ref, 0), (second_ref, 0), (pair_ref, 64))):
        node = place[level]
        for part, (ref, index) in enumerate(((inv_ref, node - 1), (off_ref, node - 2))):
            copies.append(
                pltpu.make_async_copy(
                    ref.at[index, at, :],
                    piece.at[pl.ds(start + part * 32, 32), :],
                    sems.at[len(copies)],
                )
            )
    for copy in copies:
        copy.start()
    right = leaf_ref[0].astype(BF)
    for f in range(FRONTS):
        out_ref[f, :64, :] = right
    for copy in copies:
        copy.wait()
    total = jnp.zeros((256, 256), F32)
    to = iota((256, 256), 0)
    come = iota((256, 256), 1)
    slot = to % 16
    odd = place[9].astype(F32)
    even = 1.0 - odd
    for a in range(4):
        sub = place[4 + a]
        width, start = WIDTHS[a], STARTS[a]
        from_col = (to - slot) + sub * width + (slot - start)
        chosen = (slot >= start) & (slot < start + width) & (come == from_col)
        high, low = halves(held[a])
        high = high.astype(F32)
        low = low.astype(F32)
        stacked = jnp.concatenate([high * even, high * odd, low * even, low * odd], axis=0)
        total = total + nt(jnp.where(chosen, 1.0, 0.0).astype(BF), stacked.astype(BF))
    out_ref[:, 64:, :] = total.astype(BF).reshape(16, 16, 256)


def first_payload(place, rhs_leaf, rhs_top, inv_top, off_top):
    return pl.pallas_call(
        first_kernel,
        out_shape=(
            jax.ShapeDtypeStruct((FRONTS, 80, 256), BF),
            jax.ShapeDtypeStruct((64, 1024), BF),
            jax.ShapeDtypeStruct((128, 1024), BF),
        ),
        in_specs=[SMEM, VMEM, HBM, HBM, HBM],
        out_specs=(VMEM,) * 3,
        scratch_shapes=[pltpu.VMEM((4, 64, 256), F32), pltpu.SemaphoreType.DMA((10,))],
        compiler_params=params(60),
    )(place, rhs_leaf, rhs_top, inv_top, off_top)


def stack_kernel(start, *refs):
    for k, ref in enumerate(refs[:-1]):
        refs[-1][k * 64 : (k + 1) * 64, :] = ref[start : start + 64, :]


def stack(parts, start):
    return call(
        functools.partial(stack_kernel, start),
        jax.ShapeDtypeStruct((256, 1024), BF),
        [VMEM] * 4,
        tuple(parts),
    )


def turn(block, dx, dy):
    route = [(i, (i // 4 + dx) % 4 * 4 + (i % 4 + dy) % 4) for i in range(FRONTS)]
    return lax.ppermute(block, "front", route)


def step_of(axis):
    return (1, 0) if axis == "x" else (0, 1)


def near(block, axis):
    dx, dy = step_of(axis)
    return turn(block, dx, dy), turn(block, -dx, -dy)


def opposite(block, axis):
    dx, dy = step_of(axis)
    return turn(block, 2 * dx, 2 * dy)


def far(pair, axis):
    dx, dy = step_of(axis)
    before, after = pair
    half = before.shape[0] // 2
    return turn(after[:half], -dx, -dy), turn(before[half:], dx, dy)


def leaf_solve_kernel(inv_ref, rhs_ref, off_ref, x_ref, out_ref):
    right = rhs_ref[:, :64, :].reshape(1024, 256)
    x = nn(inv_ref[0], right)
    x_ref[...] = x
    xt = x.T.astype(BF)
    update = nn(xt, off_ref[0])
    out_ref[...] = update.astype(BF).reshape(16, 16, 1024)


def push(update, idx, count):
    high, low = halves(update)
    both = jnp.concatenate([high, low], axis=0)
    blocks = []
    step = 512
    for a in range(count):
        parts = []
        for t in range(1024 // step):
            hit = iota((step, 1024), 0) + (a * 1024 + t * step) == idx
            got = nt(both, jnp.where(hit, 1.0, 0.0).astype(BF))
            parts.append(got[:16] + got[16:])
        blocks.append(jnp.concatenate(parts, axis=1))
    return blocks


def leaf_update_kernel(place, first_ref, got_ref, idx_ref, next_ref, rest_ref):
    update = jnp.zeros((16, 1024), F32)
    for s in range(FRONTS):
        update = update + got_ref[s].astype(F32)
    pending = push(update, idx_ref[...], 4)
    high, low = [], []
    for g in range(FRONTS // 2):
        pair = first_ref[2 * g, 64:, :].astype(F32) + first_ref[2 * g + 1, 64:, :].astype(F32)
        high.append(pair[:, :128])
        low.append(pair[:, 128:])
    high = jnp.concatenate(high, axis=1).astype(BF)
    low = jnp.concatenate(low, axis=1).astype(BF)
    row = iota((16, 16), 0)
    slot = iota((16, 16), 1)
    for a in range(4):
        width, start = WIDTHS[a], STARTS[a]
        put = (slot >= start) & (slot < start + width)
        put = put & (row == place[4 + a] * width + slot - start)
        put = jnp.where(put, 1.0, 0.0).astype(BF)
        block = nn(put, high) + nn(put, low) - pending[a]
        if a == 0:
            next_ref[...] = block
        else:
            rest_ref[(a - 1) * 16 : a * 16, :] = block


def solve_kernel(own_ref, other_ref, *refs):
    weights, ux_ref = refs[:-1], refs[-1]
    right = (own_ref[...] + other_ref[...]).astype(BF)
    update = jnp.zeros((16, 1024), F32)
    at = 1024
    for ref in weights:
        rows = ref.shape[0] * 32
        x = nt(right, ref[:, :32, :].reshape(rows, 1024))
        update = update + nn(x.astype(BF), ref[:, 32:, :].reshape(rows, 1024))
        ux_ref[:, at : at + rows] = x
        at += rows
    ux_ref[:, :1024] = update


def top_solve(own, other, weights):
    weights = [part.reshape(-1, 64, 1024) for part in weights]
    return call(
        solve_kernel,
        jax.ShapeDtypeStruct((16, 1536), F32),
        [VMEM] * (2 + len(weights)),
        (own, other, *weights),
    )


def update_kernel(level, place, own_ref, other_ref, left_ref, left_other_ref, idx_ref, *outs):
    update = own_ref[:, :1024] + other_ref[:, :1024]
    count = left_ref.shape[0] // 16
    idx = idx_ref[pl.ds(place[level] - 2, 1), :]
    for a, block in enumerate(push(update, idx, count)):
        at = slice(a * 16, (a + 1) * 16)
        block = left_ref[at, :] + left_other_ref[at, :] - block
        if a == 0:
            outs[0][...] = block
        else:
            outs[1][(a - 1) * 16 : a * 16, :] = block


def top_update(level, place, ux, ux_other, left, left_other, idx_top):
    shapes = [jax.ShapeDtypeStruct((16, 1024), F32)]
    if left.shape[0] > 16:
        shapes.append(jax.ShapeDtypeStruct((left.shape[0] - 16, 1024), F32))
    return call(
        functools.partial(update_kernel, level),
        tuple(shapes),
        [SMEM] + [VMEM] * 5,
        (place, ux, ux_other, left, left_other, idx_top),
    )


def ship_kernel(order, place, own_ref, other_ref, out_ref):
    first = place[8] == 0
    own = own_ref[:, 1024:]
    other = other_ref[:, 1024:]
    low_core = jnp.where(first, own, other)
    high_core = jnp.where(first, other, own)
    for k in range(FRONTS):
        outer, inner = (0, 3, 1, 2)[k // 4], (0, 3, 1, 2)[k % 4]
        if order == "yx":
            to = (place[10] + outer) % 4 * 4 + (place[11] + inner) % 4
        else:
            to = (place[10] + inner) % 4 * 4 + (place[11] + outer) % 4
        at = slice(k * 32, (k + 1) * 32)
        value = jnp.concatenate([low_core[:, at], high_core[:, at]], axis=1)
        high = value.astype(BF).astype(F32)
        low = value - high
        out_ref[to] = jnp.concatenate([high, low], axis=1).astype(BF)


def root_right_kernel(own_ref, other_ref, s3_ref, s2_ref, s1_ref, out_ref):
    right = (own_ref[...] + other_ref[...]).astype(BF)
    for f in range(FRONTS):
        out_ref[f, :, :1024] = right
    out_ref[:, :, 1024:1152] = s3_ref[...]
    out_ref[:, :, 1152:1280] = s2_ref[...]
    out_ref[:, :, 1280:] = s1_ref[...]


def root_kernel(got_ref, inv_ref, out_ref):
    right = got_ref[:, :, :1024].reshape(256, 1024)
    out_ref[3] = nt(inv_ref[0], right)
    for a in range(3):
        at = 1024 + a * 128
        both = got_ref[:, :, at : at + 128].reshape(256, 128).astype(F32).T
        out_ref[a] = both[:64] + both[64:]


def swap(block, pairs):
    return lax.ppermute(block, "leaf", pairs)


def core_pairs():
    return [(i, i ^ 1) for i in range(16)]


def chip_pairs(level):
    pairs = []
    for i in range(16):
        z, core = i // 2, i % 2
        if level == 0:
            to = z ^ 1
        elif level == 1:
            to = z ^ 2
        else:
            to = (6, 7, 4, 5, 2, 3, 0, 1)[z]
        pairs.append((i, 2 * to + core))
    return pairs


def local(rhs_leaf, rhs_top, inv_leaf, inv_top, off_leaf, off_top, idx_leaf, idx_top):
    leaf = lax.axis_index("leaf")
    front = lax.axis_index("front")
    nodes = [jnp.right_shift(16 + leaf, a + 1) for a in range(4)]
    subs = [leaf & (2 ** (a + 1) - 1) for a in range(4)]
    place = nodes + subs + [leaf & 1, front & 1, front // 4, front % 4]
    place = jnp.stack(place).astype(jnp.int32)
    off_top = jnp.swapaxes(off_top, 1, 2)
    off_leaf = jnp.swapaxes(off_leaf, 1, 2)

    sent, second, pair = first_payload(place, rhs_leaf, rhs_top, inv_top, off_top)
    first = lax.all_to_all(sent, "front", 0, 0)
    pair = (pair, *near(pair, "y"))
    pair = (*pair, opposite(pair[0], "y"))
    second = (second, *near(second, "x"), opposite(second, "x"))
    leaf_x, sent = call(
        leaf_solve_kernel,
        (jax.ShapeDtypeStruct((64, 256), F32), jax.ShapeDtypeStruct((FRONTS, 16, 1024), BF)),
        [VMEM] * 3,
        (inv_leaf, first, off_leaf),
    )
    sent, pair, second = lax.optimization_barrier((sent, pair, second))
    got = lax.all_to_all(sent, "front", 0, 0)
    third, second = stack(pair, 0), stack(second, 0)
    third_near = near(third, "x")
    got, third_near, second, pair = lax.optimization_barrier((got, third_near, second, pair))
    second_near = near(second, "y")
    lowest = stack(pair, 64)
    third_far = far(third_near, "x")
    state, left = call(
        leaf_update_kernel,
        (jax.ShapeDtypeStruct((16, 1024), F32), jax.ShapeDtypeStruct((48, 1024), F32)),
        [SMEM] + [VMEM] * 3,
        (place, first, got, idx_leaf),
    )
    second_far = far(second_near, "y")
    other, left_other = swap(state, core_pairs()), swap(left, core_pairs())
    ships = []
    for level in range(3):
        if level == 0:
            parts = (third, *third_near, *third_far)
        elif level == 1:
            parts = (second, *second_near, *second_far)
        else:
            parts = (lowest, *lowest_near, *lowest_far)
        ux = top_solve(state, other, parts)
        if level == 0:
            ux, lowest = lax.optimization_barrier((ux, lowest))
            lowest_near = near(lowest, "x")
        if level > 0:
            ux, left_other = lax.optimization_barrier((ux, left_other))
        ux_other = swap(ux, core_pairs())
        state, *more = top_update(level, place, ux, ux_other, left, left_other, idx_top)
        other = swap(state, chip_pairs(level))
        if level == 0:
            other, lowest_near = lax.optimization_barrier((other, lowest_near))
            lowest_far = far(lowest_near, "x")
        if more:
            left, left_other = more[0], swap(more[0], chip_pairs(level))
        ships.append(
            call(
                functools.partial(ship_kernel, ("yx", "xy", "yx")[level]),
                jax.ShapeDtypeStruct((16, 16, 128), BF),
                [SMEM, VMEM, VMEM],
                (place, ux, ux_other),
            )
        )
    sent = call(
        root_right_kernel,
        jax.ShapeDtypeStruct((16, 16, 1408), BF),
        [VMEM] * 5,
        (state, other, *ships),
    )
    got = lax.all_to_all(sent, "front", 0, 0)
    ancestors = call(
        root_kernel,
        jax.ShapeDtypeStruct((4, 64, 256), F32),
        [VMEM] * 2,
        (got, inv_top[:1]),
    )
    return (leaf_x[None], ancestors[None])


def solution(mesh):
    placed = (
        P("leaf", "front", None),
        P(None, "front", None),
        P("leaf", "front", None),
        P(None, "front", None),
        P("leaf", None, "front"),
        P(None, None, "front"),
        P("leaf", None),
        P(),
    )
    return jax.shard_map(
        local,
        mesh=mesh,
        in_specs=placed,
        out_specs=(P("leaf", "front", None), P("leaf", None, "front", None)),
        check_vma=False,
    )
```
